256 devices in a mesh: fsdp: 128 (over y, x, z), rep: 2 (over core).
Axes of the slice: x: 4, y: 4, z: 8, core: 2. Of those that a mesh axis runs over, the one named last changes fastest.
Arguments:
- gradient: bfloat16 [2, 8, 4096, 4096], P('rep', None, 'fsdp'), may hold values from -80 to 80
- old_stats: float32 [2, 512, 512, 512], P('rep', 'fsdp'), may hold values from -1 to 8192, as said below
- owner_table: int32 [128, 4], replicated, may hold values from 0 to 511, as said below
Outputs:
- update: bfloat16 [8, 4096, 4096], P(None, 'fsdp')
- new_stats: float32 [2, 512, 512, 512], P('rep', 'fsdp')
The draws below stay inside these ranges and needn't reach their ends.
Inputs may be any that keep to these rules, and one draw needn't show every extreme that they name: Every block number appears exactly once. The four entries of one row of owner_table name blocks of four different row groups ((b // 8) % 8). Each old_stats[r, s] is symmetric positive definite.
All inputs are finite; a program needn't handle non-finite values.
Results may differ from the reference program's by a relative error of at most 0.0078.
Values may be sent and summed in bfloat16 or wider, within the bound.
A program may use at most 128 MiB of HBM per device.

```python
import math
import jax
import jax.numpy as jnp
from jax import lax

D = 4096
BLOCK_ORDER = 512
NMAT = 8
ITERS = 2
DATA_REPLICAS = 2
ROWS = 4096
COLB = 8
GROUPS = 8
NBLK = 512
SLOTS = 4
OWNER_SLOT_COUNT = 512
N_FSDP = 128


def draw_gradient(key, part):
    key = jax.random.fold_in(key, 11)
    random_subkeys = jax.random.split(key, 3)
    full_shape = (DATA_REPLICAS, NMAT, ROWS, D)
    row_scale = jnp.exp(jax.random.uniform(random_subkeys[0], (1, NMAT, ROWS, 1), jnp.float32, math.log(0.3), math.log(3.0)))
    col_scale = jnp.exp(jax.random.uniform(random_subkeys[1], (1, NMAT, 1, D), jnp.float32, math.log(0.3), math.log(3.0)))
    position = jnp.arange(ROWS, dtype=jnp.float32)[None, None, :, None] / ROWS
    rising = 3.0 ** (0.5 * position)
    values = jax.random.truncated_normal(random_subkeys[2], -4.0, 4.0, full_shape, jnp.float32)
    return (values * row_scale * col_scale * rising).astype(jnp.bfloat16)


def draw_old_stats(key, part):
    key = jax.random.fold_in(key, 23)
    random_subkeys = jax.random.split(key, 2)
    spread_factor = jax.random.uniform(random_subkeys[0], (DATA_REPLICAS, OWNER_SLOT_COUNT, BLOCK_ORDER, BLOCK_ORDER), jnp.float32, -1.0, 1.0)
    symmetric = 0.5 * (spread_factor + jnp.swapaxes(spread_factor, 2, 3))
    identity = jnp.eye(BLOCK_ORDER, dtype=jnp.float32)
    lower_bound = 1.0
    upper_bound = 8.0
    diagonal_entries = BLOCK_ORDER * jnp.exp(jax.random.uniform(random_subkeys[1], (DATA_REPLICAS, OWNER_SLOT_COUNT, BLOCK_ORDER, 1), jnp.float32, math.log(lower_bound), math.log(upper_bound)))
    return symmetric * (1.0 - identity) + diagonal_entries * identity


def draw_owner_table(key, part):
    key = jax.random.fold_in(key, 37)
    random_subkeys = jax.random.split(key, 2)
    total_slots = N_FSDP * SLOTS
    shuffled = jax.random.permutation(random_subkeys[0], N_FSDP).astype(jnp.int32)
    offset = shuffled % GROUPS
    row_group = (offset[:, None] + jnp.arange(SLOTS, dtype=jnp.int32)[None, :]) % GROUPS
    flat_group = row_group.reshape(-1)
    tiebreak = jax.random.permutation(random_subkeys[1], total_slots).astype(jnp.int32)
    scores = flat_group * total_slots + tiebreak
    ordering = jnp.argsort(scores, stable=True).astype(jnp.int32)
    ranking = jnp.zeros((total_slots,), jnp.int32).at[ordering].set(jnp.arange(total_slots, dtype=jnp.int32))
    per_group = total_slots // GROUPS
    within = ranking - flat_group * per_group
    matrix_index = within // COLB
    column_index = within % COLB
    blocks = (matrix_index * GROUPS + flat_group) * COLB + column_index
    return blocks.reshape(N_FSDP, SLOTS).astype(jnp.int32)


def setup_inputs(seed: int = 0) -> dict:
    key_list = jax.random.split(jax.random.key(seed), 4)
    gradient = draw_gradient(jax.random.fold_in(key_list[3], 71), 0)
    old_stats = draw_old_stats(jax.random.fold_in(key_list[3], 71), 0)
    owner_table = draw_owner_table(jax.random.fold_in(key_list[3], 71), 0)
    return dict(gradient=gradient, old_stats=old_stats, owner_table=owner_table)


DECAY_RATE = 0.95
EPSILON = 1e-06

def dot_full(left_mat, right_mat):
    return jnp.dot(left_mat, right_mat, precision=lax.Precision.HIGHEST, preferred_element_type=jnp.float32)

def inverse_root(statistic):
    order_size = statistic.shape[0]
    identity = jnp.eye(order_size, dtype=jnp.float32)
    frobenius = jnp.sqrt(jnp.sum(statistic * statistic) + EPSILON)
    moment = statistic / frobenius
    factor = (5.0 * identity - moment) * 0.25
    root_now = factor * frobenius ** (-0.25)
    for repeat in range(ITERS - 1):
        square = dot_full(factor, factor)
        fourth = dot_full(square, square)
        moment = dot_full(fourth, moment)
        factor = (5.0 * identity - moment) * 0.25
        root_now = dot_full(root_now, factor)
    return root_now

def reference(gradient, old_stats, owner_table):
    grad_sum = lax.optimization_barrier(jnp.sum(gradient.astype(jnp.float32), axis=0)).astype(jnp.bfloat16)
    block_grid = grad_sum.reshape(NMAT, GROUPS, BLOCK_ORDER, COLB, BLOCK_ORDER).transpose(0, 1, 3, 2, 4).reshape(NBLK, BLOCK_ORDER, BLOCK_ORDER)
    flat_table = owner_table.reshape(-1).astype(jnp.int32)
    slot_blocks = block_grid[flat_table]

    def one_slot(inputs):
        block_now, left_old, right_old = inputs
        left_stat = DECAY_RATE * left_old + jnp.dot(block_now, block_now.T, preferred_element_type=jnp.float32)
        right_stat = DECAY_RATE * right_old + jnp.dot(block_now.T, block_now, preferred_element_type=jnp.float32)
        left_root = inverse_root(left_stat).astype(jnp.bfloat16)
        right_root = inverse_root(right_stat).astype(jnp.bfloat16)
        right_part = jnp.dot(block_now, right_root, preferred_element_type=jnp.float32).astype(jnp.bfloat16)
        precond = jnp.dot(left_root, right_part, preferred_element_type=jnp.float32).astype(jnp.bfloat16)
        return (left_stat, right_stat, precond)
    left_all, right_all, precond_all = lax.map(one_slot, (slot_blocks, old_stats[0], old_stats[1]))
    placed = jnp.zeros((NBLK, BLOCK_ORDER, BLOCK_ORDER), jnp.bfloat16).at[flat_table].set(precond_all)
    precond_rows = placed.reshape(NMAT, GROUPS, COLB, BLOCK_ORDER, BLOCK_ORDER).transpose(0, 1, 3, 2, 4).reshape(NMAT, ROWS, D)
    grad_wide = grad_sum.astype(jnp.float32)
    prec_wide = precond_rows.astype(jnp.float32)
    grad_sq = lax.optimization_barrier(jnp.sum(grad_wide * grad_wide, axis=(1, 2)))
    prec_sq = lax.optimization_barrier(jnp.sum(prec_wide * prec_wide, axis=(1, 2)))
    entry_count = ROWS * D
    graft_scale = jnp.sqrt((grad_sq / entry_count + EPSILON) / (prec_sq / entry_count + EPSILON))
    update = (prec_wide * graft_scale[:, None, None]).astype(jnp.bfloat16)
    return (update, jnp.stack([left_all, right_all]))
```

```python
import functools

import jax
import jax.numpy as jnp
from jax import lax
from jax.experimental import pallas as pl
from jax.experimental.pallas import tpu as pltpu
from jax.sharding import PartitionSpec as P

DECAY_RATE = 0.95
EPSILON = 1e-06
MESH = pl.DeviceIdType.MESH
F32 = jnp.float32
BF16 = jnp.bfloat16
VMEM_BYTES = 50 * 1024 * 1024

DEPTH = 8

COEF = tuple(
    v / 4096.0 for v in (6400.0, -4405.0, 3125.0, -1250.0, 250.0, -25.0, 1.0)
)


def steps_of(depth):
    order = []
    for low in range(depth // 2 - 1, 0, -1):
        order += [low, depth - low]
    order = order[:2] + [depth // 2] + order[2:] + [0]
    width = 2 if depth % 2 == 0 else 1
    return [order[at : at + width] for at in range(0, depth, width)]


class Plan:
    def __init__(self, fsdp, matrices, slab, model, slots, block):
        self.fsdp, self.matrices, self.slab, self.model = fsdp, matrices, slab, model
        self.slots, self.block = slots, block
        self.depth = DEPTH
        self.lines = fsdp // self.depth
        self.columns = model // block
        self.span = block // slab
        self.groups = fsdp // self.span
        self.tall = self.span // self.depth
        self.half = slab // 2
        self.out_steps = steps_of(self.depth)
        self.back_steps = [list(reversed(pair)) for pair in reversed(self.out_steps)]
        self.pairs = len(self.out_steps)
        self.width = len(self.out_steps[0])


def dot(a, b, dims=((1,), (0,))):
    return lax.dot_general(a, b, (dims, ((), ())), preferred_element_type=F32)


def fold(rows):
    line = jnp.sum(rows, axis=0, keepdims=True)
    total = line[:, :128]
    for at in range(128, line.shape[1], 128):
        total = total + line[:, at : at + 128]
    return total


def kernel(p, tab, grad, old, upd, new, *scratch):
    (mine, theirs, gsum, send_a, land_a, send_b, blocks, stat, root, other, half_out) = scratch[:11]
    (land_c, send_d, land_d, made, sums, wide, sums_z, sums_l, sums_c) = scratch[11:20]
    (load_g, load_o, save_n, save_u, pair_s, pair_r, a_s, a_r, b_s, b_r) = scratch[20:30]
    (x_s, x_r, root_s, root_r, c_s, c_r, d_s, d_r, y_s, y_r) = scratch[30:40]
    (qz_s, qz_r, ql_s, ql_r, qc_s, qc_r) = scratch[40:]

    depth, lines, slots, block = p.depth, p.lines, p.slots, p.block
    half, tall, columns = p.half, p.tall, p.columns
    me = lax.axis_index("fsdp")
    core = lax.axis_index("rep")
    far_core = 1 - core
    line = me // depth
    place = me % depth
    partner = (me, far_core)

    def at(other_line, other_place):
        return (other_line * depth + other_place, core)

    def remote(src, dst, send, recv, device):
        return pltpu.make_async_remote_copy(
            src_ref=src, dst_ref=dst, send_sem=send, recv_sem=recv,
            device_id=device, device_id_type=MESH,
        )

    def landed(ref, sem):
        pltpu.make_async_copy(ref, ref, sem).wait()

    my_rows = pl.ds(pl.multiple_of(core * half, half), half)
    far_rows = pl.ds(pl.multiple_of(far_core * half, half), half)

    barrier = pltpu.get_barrier_semaphore()

    def greet(device):
        pl.semaphore_signal(barrier, inc=1, device_id=device, device_id_type=MESH)

    greet(partner)

    @pl.loop(1, depth)
    def _(step):
        greet(at(line, (place + step) % depth))

    @pl.loop(1, lines)
    def _(step):
        greet(at((line + step) % lines, place))

    parts = 4
    per = p.matrices // parts
    for i in range(parts):
        m = pl.ds(i * per, per)
        pltpu.make_async_copy(grad.at[0, m, my_rows, :], mine.at[m], load_g.at[i]).start()
    for j in range(slots):
        pltpu.make_async_copy(old.at[0, j], stat.at[j], load_o.at[j]).start()
    sums[...] = jnp.zeros_like(sums)
    pl.semaphore_wait(barrier, depth + lines - 1)

    for i in range(parts):
        m = pl.ds(i * per, per)
        remote(grad.at[0, m, far_rows, :], theirs.at[m], pair_s.at[i], pair_r.at[i], partner).start()
    for i in range(parts):
        m = pl.ds(i * per, per)
        landed(mine.at[m], load_g.at[i])
        landed(theirs.at[m], pair_r.at[i])

        @pl.loop(i * per, (i + 1) * per)
        def _(m):
            square = jnp.zeros((half, block), F32)
            for c in range(columns):
                cut = slice(c * block, (c + 1) * block)
                value = (mine[m, :, cut].astype(F32) + theirs[m, :, cut].astype(F32)).astype(BF16)
                gsum[m * columns + c] = value
                value = value.astype(F32)
                square = square + value * value
            sums[0, pl.ds(m, 1), :] = fold(square)

    for a, pair in enumerate(p.out_steps):

        @pl.loop(0, lines)
        def _(to):
            for i, k in enumerate(pair):
                piece = gsum[tab[0, to * depth + (place + k) % depth]]
                send_a[a, to, i] = piece

        @pl.loop(1, lines)
        def _(step):
            to = (line + step) % lines
            remote(send_a.at[a, to], land_a[a].at[line], a_s.at[a], a_r.at[a], at(to, place)).start()

        for i in range(p.width):
            land_a[a][line, i] = send_a[a, line, i]

    for a, pair in enumerate(p.out_steps):
        landed(land_a[a].at[pl.ds(0, lines - 1)], a_r.at[a])
        for i, k in enumerate(pair):
            to = (place + k) % depth
            for j in range(slots):
                group = tab[1, to * slots + j]
                for t in range(tall):
                    piece = land_a[a][group * tall + t, i]
                    if k:
                        send_b[k - 1, j, t] = piece
                    else:
                        blocks[j, t, place, core] = piece
            if k:
                remote(
                    send_b.at[k - 1], blocks.at[:, :, place, core], b_s.at[k], b_r.at[k], at(line, to)
                ).start()

    for pair in p.out_steps:
        for k in pair:
            rows = blocks.at[:, :, (place + depth - k) % depth, core]
            if k:
                landed(rows, b_r.at[k])
            remote(rows, rows, x_s.at[k], x_r.at[k], partner).start()
    for pair in p.out_steps:
        for k in pair:
            landed(blocks.at[:, :, (place + depth - k) % depth, far_core], x_r.at[k])

    row_id = lax.broadcasted_iota(jnp.int32, (block, block), 0)
    col_id = lax.broadcasted_iota(jnp.int32, (block, block), 1)

    @pl.loop(0, slots)
    def _(j):
        landed(stat.at[j], load_o.at[j])

        @pl.when(core == 0)
        def _():
            g = blocks[j].reshape(block, block)
            stat[j] = DECAY_RATE * stat[j] + dot(g, g, ((1,), (1,)))

        @pl.when(core == 1)
        def _():
            g = blocks[j].reshape(block, block)
            stat[j] = DECAY_RATE * stat[j] + dot(g, g, ((0,), (0,)))

        pltpu.make_async_copy(stat.at[j], new.at[0, j], save_n.at[j]).start()
        a = stat[j]
        norm2 = jnp.sum(jnp.sum(a * a, axis=0, keepdims=True), axis=1, keepdims=True) + EPSILON
        norm = jnp.sqrt(norm2)
        m1 = a * (1.0 / norm)
        b1 = m1.astype(BF16)
        m2 = dot(b1, b1)
        b2 = m2.astype(BF16)
        m3 = dot(b1, b2)
        upper = (COEF[4] * m1 + COEF[5] * m2 + COEF[6] * m3).astype(BF16)
        lower = COEF[1] * m1 + COEF[2] * m2 + COEF[3] * m3
        lower = lower + jnp.where(row_id == col_id, COEF[0], 0.0)
        x = (lower + dot(m3.astype(BF16), upper)) * lax.rsqrt(jnp.sqrt(norm))
        root[j] = x.astype(BF16).reshape(root.shape[1:])
        remote(root.at[j], other.at[j], root_s.at[j], root_r.at[j], partner).start()

    def apply(j, left, right):
        g = blocks[j].reshape(block, block)
        part = dot(g, right[j].reshape(block, block)).astype(BF16)
        rows = left[j, :, :, core].reshape(block // 2, block)
        return dot(rows, part).astype(BF16)

    matrix_id = lax.broadcasted_iota(jnp.int32, sums.shape[1:], 0)

    @pl.loop(0, slots)
    def _(j):
        landed(other.at[j], root_r.at[j])

        @pl.when(core == 0)
        def _():
            half_out[j] = apply(j, root, other).reshape(half_out.shape[1:])

        @pl.when(core == 1)
        def _():
            half_out[j] = apply(j, other, root).reshape(half_out.shape[1:])

        value = half_out[j].reshape(block // 2, block).astype(F32)
        total = fold(value * value)
        sums[1] = sums[1] + jnp.where(matrix_id == tab[4, j], total, 0.0)

    sums_z[place] = sums[...]

    @pl.loop(1, depth)
    def _(step):
        remote(sums, sums_z.at[place], qz_s, qz_r, at(line, (place + step) % depth)).start()

    for pair in p.back_steps:
        for k in pair:
            if k:
                to = (place + depth - k) % depth
                remote(half_out.at[:, :, to], land_c[k - 1], c_s.at[k], c_r.at[k], at(line, to)).start()

    for a, pair in enumerate(p.back_steps):
        for i, k in enumerate(pair):
            if k:
                landed(land_c[k - 1], c_r.at[k])
            owner = (place + k) % depth

            @pl.loop(0, lines)
            def _(to):
                slot = tab[2, owner * p.groups + to // tall]
                if k:
                    piece = land_c[k - 1][slot, to % tall]
                else:
                    piece = half_out[slot, to % tall, place]
                send_d[a, to, i] = piece

        if a == 0:
            landed(sums_z.at[pl.ds(0, depth - 1)], qz_r)
            sums_l[line] = jnp.sum(sums_z[...], axis=0)

            @pl.loop(1, lines)
            def _(step):
                remote(sums_l.at[line], sums_l.at[line], ql_s, ql_r, at((line + step) % lines, place)).start()

        spot = pl.ds((a * lines + line) * p.width, p.width)

        @pl.loop(1, lines)
        def _(step):
            to = (line + step) % lines
            remote(send_d.at[a, to], land_d.at[core, spot], d_s.at[a], d_r.at[a], at(to, place)).start()

        land_d[core, spot] = send_d[a, line]

    landed(sums_l.at[pl.ds(0, lines - 1)], ql_r)
    sums_c[0] = jnp.sum(sums_l[...], axis=0)
    remote(sums_c.at[0], sums_c.at[1], qc_s, qc_r, partner).start()

    chunk = lines * p.width
    for a in range(p.pairs):
        landed(land_d.at[core, pl.ds(0, chunk - p.width)], d_r.at[a])
        rows = land_d.at[core, pl.ds(a * chunk, chunk)]
        remote(rows, rows, y_s.at[a], y_r.at[a], partner).start()

    landed(sums_c.at[1], qc_r)
    total = jnp.sum(sums_c[0] + sums_c[1], axis=2, keepdims=True)
    count = float(p.slab * p.fsdp * p.model)
    scale = jnp.sqrt((total[0] / count + EPSILON) / (total[1] / count + EPSILON))
    wide[...] = jnp.broadcast_to(scale, wide.shape)
    for a in range(p.pairs):
        landed(land_d.at[far_core, pl.ds(a * chunk, chunk)], y_r.at[a])

    @pl.loop(0, p.matrices)
    def _(m):
        factor = wide[pl.ds(m, 1), :]
        for c in range(columns):
            spot = tab[3, m * columns + c]
            for h in range(2):
                piece = land_d[h, spot].astype(F32) * factor
                made[m, h * half : (h + 1) * half, c * block : (c + 1) * block] = piece.astype(BF16)
        pltpu.make_async_copy(made.at[m], upd.at[m], save_u.at[m]).start()

    for i in range(parts):
        landed(theirs.at[pl.ds(i * per, per)], pair_s.at[i])
    for a in range(p.pairs):
        landed(send_a.at[a, pl.ds(0, lines - 1)], a_s.at[a])
        landed(send_d.at[a, pl.ds(0, lines - 1)], d_s.at[a])
        landed(land_d.at[core, pl.ds(a * chunk, chunk)], y_s.at[a])
    for k in range(depth):
        landed(blocks.at[:, :, (place + depth - k) % depth, core], x_s.at[k])
        if k:
            landed(send_b.at[k - 1], b_s.at[k])
            landed(land_c[k - 1], c_s.at[k])
    for j in range(slots):
        landed(root.at[j], root_s.at[j])
        landed(stat.at[j], save_n.at[j])
    landed(sums_z.at[pl.ds(0, depth - 1)], qz_s)
    landed(sums_l.at[pl.ds(0, lines - 1)], ql_s)
    landed(sums_c.at[0], qc_s)
    for m in range(p.matrices):
        landed(made.at[m], save_u.at[m])


def tables(p, owner_table):
    me = lax.axis_index("fsdp")
    line, place = me // p.depth, me % p.depth
    my_group = me // p.span
    groups, columns = p.groups, p.columns
    group_of = owner_table // columns % groups
    matrix_of = owner_table // (columns * groups)
    local = matrix_of * columns + owner_table % columns
    here = group_of == my_group
    first = jnp.sum(jnp.where(here, local, 0), axis=1)
    on_line = lax.dynamic_slice_in_dim(group_of, line * p.depth, p.depth, 0)
    second = on_line.reshape(-1)
    slot = jnp.arange(p.slots, dtype=jnp.int32)
    hits = on_line[:, :, None] == jnp.arange(groups, dtype=jnp.int32)[None, None, :]
    third = jnp.sum(jnp.where(hits, slot[None, :, None], 0), axis=1).reshape(-1)
    spot = [0] * p.depth
    for a, pair in enumerate(p.back_steps):
        for i, k in enumerate(pair):
            spot[k] = a * p.lines * p.width + i
    owner = jnp.arange(p.fsdp, dtype=jnp.int32)
    gap = (owner % p.depth - place) % p.depth
    land = owner // p.depth * p.width
    for k in range(p.depth):
        land = land + jnp.where(gap == k, spot[k], 0)
    wanted = jnp.arange(p.matrices * columns, dtype=jnp.int32)
    match = here[None] & (local[None] == wanted[:, None, None])
    fourth = jnp.sum(jnp.where(match, land[None, :, None], 0), axis=(1, 2))
    fifth = lax.dynamic_slice_in_dim(matrix_of, me, 1, 0).reshape(-1)
    rows = [jnp.pad(row, (0, 128 - row.shape[0])) for row in (first, second, third, fourth, fifth)]
    return jnp.stack(rows)


def body(p, gradient, old_stats, owner_table):
    tab = tables(p, owner_table)
    depth, lines, slots, block = p.depth, p.lines, p.slots, p.block
    half, tall, pairs, width = p.half, p.tall, p.pairs, p.width
    dma = pltpu.SemaphoreType.DMA
    vm = pltpu.VMEM
    full = (slots, tall, depth, 2, half, block)
    scratch = [
        vm((p.matrices, half, p.model), BF16),
        vm((p.matrices, half, p.model), BF16),
        vm((p.matrices * p.columns, half, block), BF16),
        vm((pairs, lines, width, half, block), BF16),
        [vm((lines, width, half, block), BF16) for _ in range(pairs)],
        vm((depth - 1, slots, tall, half, block), BF16),
        vm(full, BF16),
        vm((slots, block, block), F32),
        vm(full, BF16),
        vm(full, BF16),
        vm((slots, tall, depth, half, block), BF16),
        [vm((slots, tall, half, block), BF16) for _ in range(depth - 1)],
        vm((pairs, lines, width, half, block), BF16),
        vm((2, pairs * lines * width, half, block), BF16),
        vm((p.matrices, p.slab, p.model), BF16),
        vm((2, p.matrices, 128), F32),
        vm((p.matrices, block), F32),
        vm((depth, 2, p.matrices, 128), F32),
        vm((lines, 2, p.matrices, 128), F32),
        vm((2, 2, p.matrices, 128), F32),
    ]
    counts = [4, slots, slots, p.matrices, 4, 4, pairs, pairs, depth, depth]
    counts += [depth, depth, slots, slots, depth, depth, pairs, pairs, pairs, pairs]
    scratch += [dma((count,)) for count in counts]
    scratch += [dma] * 6
    update, fresh = pl.pallas_call(
        functools.partial(kernel, p),
        out_shape=(
            jax.ShapeDtypeStruct((p.matrices, p.slab, p.model), BF16),
            jax.ShapeDtypeStruct(old_stats.shape, F32),
        ),
        in_specs=[
            pl.BlockSpec(memory_space=pltpu.SMEM),
            pl.BlockSpec(memory_space=pl.ANY),
            pl.BlockSpec(memory_space=pl.ANY),
        ],
        out_specs=(pl.BlockSpec(memory_space=pl.ANY), pl.BlockSpec(memory_space=pl.ANY)),
        scratch_shapes=scratch,
        compiler_params=pltpu.CompilerParams(
            collective_id=0, has_side_effects=True, vmem_limit_bytes=VMEM_BYTES
        ),
        name="shampoo",
    )(tab, gradient, old_stats)
    return update, fresh


def solution(mesh):
    def whole(gradient, old_stats, owner_table):
        fsdp = mesh.shape["fsdp"]
        _, matrices, rows, model = gradient.shape
        p = Plan(fsdp, matrices, rows // fsdp, model, owner_table.shape[1], old_stats.shape[2])
        return jax.shard_map(
            functools.partial(body, p),
            mesh=mesh,
            in_specs=(P("rep", None, "fsdp", None), P("rep", "fsdp", None, None), P()),
            out_specs=(P(None, "fsdp", None), P("rep", "fsdp", None, None)),
            check_vma=False,
        )(gradient, old_stats, owner_table)

    return whole
```

```python
import functools

import jax
import jax.numpy as jnp
from jax import lax
from jax.experimental import pallas as pl
from jax.experimental.pallas import tpu as pltpu
from jax.sharding import PartitionSpec as P

DECAY_RATE = 0.95
EPSILON = 1e-06
MESH = pl.DeviceIdType.MESH
F32 = jnp.float32
BF16 = jnp.bfloat16
VMEM_BYTES = 44 * 1024 * 1024

DEPTH = 8
GROUP_ROW, SLOT_ROW = 8, 16
AHEAD = 2

COEF = tuple(
    v / 4096.0 for v in (6400.0, -4405.0, 3125.0, -1250.0, 250.0, -25.0, 1.0)
)


def steps_of(depth):
    pairs = [[low, depth - low] for low in range(depth // 2 - 1, 0, -1)]
    return [[depth // 2]] + pairs + [[0]]


class Plan:
    def __init__(self, fsdp, matrices, slab, model, slots, block):
        self.fsdp, self.matrices, self.slab, self.model = fsdp, matrices, slab, model
        self.slots, self.block = slots, block
        self.depth = DEPTH
        self.lines = fsdp // self.depth
        self.columns = model // block
        self.span = block // slab
        self.groups = fsdp // self.span
        self.tall = self.span // self.depth
        self.half = slab // 2
        self.out_steps = steps_of(self.depth)
        self.back_steps = [list(reversed(pair)) for pair in reversed(self.out_steps)]
        self.pairs = len(self.out_steps)
        self.land_row = SLOT_ROW + self.groups
        self.matrix_row = self.land_row + matrices * self.columns
        self.table_rows = -(-(self.matrix_row + slots) // 8) * 8
        self.start = [self.lines * sum(map(len, self.back_steps[:a])) for a in range(self.pairs)]


def dot(a, b, dims=((1,), (0,))):
    return lax.dot_general(a, b, (dims, ((), ())), preferred_element_type=F32)


def fold(rows):
    line = jnp.sum(rows, axis=0, keepdims=True)
    total = line[:, :128]
    for at in range(128, line.shape[1], 128):
        total = total + line[:, at : at + 128]
    return total


def kernel(p, owners, grad, old, upd, new, *scratch):
    (mine, theirs, gsum, send_a, land_a, send_b, blocks, eye, root, other, half_out) = scratch[:11]
    (land_c, send_d, land_d, sums, wide, sums_z, sums_l, sums_c, draft, tab, stat, made, listed) = scratch[11:24]
    (load_g, load_o, save_n, save_u, pair_s, pair_r, a_s, a_r, b_s, b_r) = scratch[24:34]
    (x_s, x_r, root_s, root_r, c_s, c_r, d_s, d_r, y_s, y_r) = scratch[34:44]
    (qz_s, qz_r, ql_s, ql_r, qc_s, qc_r, tab_s, list_s) = scratch[44:]

    depth, lines, slots, block = p.depth, p.lines, p.slots, p.block
    half, tall, columns = p.half, p.tall, p.columns
    me = lax.axis_index("fsdp")
    core = lax.axis_index("rep")
    far_core = 1 - core
    line = me // depth
    place = me % depth
    partner = (me, far_core)

    def at(other_line, other_place):
        return (other_line * depth + other_place, core)

    def remote(src, dst, send, recv, device):
        return pltpu.make_async_remote_copy(
            src_ref=src, dst_ref=dst, send_sem=send, recv_sem=recv,
            device_id=device, device_id_type=MESH,
        )

    def landed(ref, sem):
        pltpu.make_async_copy(ref, ref, sem).wait()

    my_rows = pl.ds(pl.multiple_of(core * half, half), half)
    far_rows = pl.ds(pl.multiple_of(far_core * half, half), half)

    barrier = pltpu.get_barrier_semaphore()

    def greet(device):
        pl.semaphore_signal(barrier, inc=1, device_id=device, device_id_type=MESH)

    greet(partner)

    @pl.loop(1, depth)
    def _(step):
        greet(at(line, (place + step) % depth))

    @pl.loop(1, lines)
    def _(step):
        greet(at((line + step) % lines, place))

    listing = pltpu.make_async_copy(owners, listed, list_s)
    listing.start()
    parts = 4
    per = p.matrices // parts
    for i in range(parts):
        m = pl.ds(i * per, per)
        pltpu.make_async_copy(grad.at[0, m, my_rows, :], mine.at[m], load_g.at[i]).start()
    for j in range(slots):
        pltpu.make_async_copy(old.at[0, j], stat.at[j], load_o.at[j]).start()
    sums[...] = jnp.zeros_like(sums)
    listing.wait()
    lookup = tables(p, listed[...], me, line, place)
    for row, value in lookup:
        draft[row : row + value.shape[0], :] = value
    pltpu.make_async_copy(draft, tab, tab_s).start()
    row_id = lax.broadcasted_iota(jnp.int32, (block, block), 0)
    col_id = lax.broadcasted_iota(jnp.int32, (block, block), 1)
    eye[...] = jnp.where(row_id == col_id, COEF[0], 0.0)
    pl.semaphore_wait(barrier, depth + lines - 1)

    for i in range(parts):
        m = pl.ds(i * per, per)
        remote(grad.at[0, m, far_rows, :], theirs.at[m], pair_s.at[i], pair_r.at[i], partner).start()
    for i in range(parts):
        m = pl.ds(i * per, per)
        landed(mine.at[m], load_g.at[i])
        landed(theirs.at[m], pair_r.at[i])

        @pl.loop(i * per, (i + 1) * per)
        def _(m):
            square = jnp.zeros((half, block), F32)
            for c in range(columns):
                cut = slice(c * block, (c + 1) * block)
                value = (mine[m, :, cut].astype(F32) + theirs[m, :, cut].astype(F32)).astype(BF16)
                gsum[m * columns + c] = value
                value = value.astype(F32)
                square = square + value * value
            sums[0, pl.ds(m, 1), :] = fold(square)

    landed(tab, tab_s)

    def across(a, pair):
        @pl.loop(0, lines)
        def _(to):
            for i, k in enumerate(pair):
                piece = gsum[tab[0, to * depth + (place + k) % depth]]
                send_a[a][to, i] = piece

        @pl.loop(1, lines)
        def _(step):
            to = (line + step) % lines
            remote(send_a[a].at[to], land_a[a].at[line], a_s.at[a], a_r.at[a], at(to, place)).start()

        for i in range(len(pair)):
            land_a[a][line, i] = send_a[a][line, i]

    def along(a, pair):
        landed(land_a[a].at[pl.ds(0, lines - 1)], a_r.at[a])
        for i, k in enumerate(pair):
            to = (place + k) % depth
            for j in range(slots):
                group = tab[GROUP_ROW + j, line * depth + to]
                for t in range(tall):
                    piece = land_a[a][group * tall + t, i]
                    if k:
                        send_b[k - 1, j, t] = piece
                    else:
                        blocks[j, t, place, core] = piece
            if k:
                remote(
                    send_b.at[k - 1], blocks.at[:, :, place, core], b_s.at[k], b_r.at[k], at(line, to)
                ).start()

    for a in range(p.pairs + AHEAD):
        if a < p.pairs:
            across(a, p.out_steps[a])
        if a >= AHEAD:
            along(a - AHEAD, p.out_steps[a - AHEAD])

    for pair in p.out_steps:
        for k in pair:
            rows = blocks.at[:, :, (place + depth - k) % depth, core]
            if k:
                landed(rows, b_r.at[k])
            remote(rows, rows, x_s.at[k], x_r.at[k], partner).start()
    for pair in p.out_steps:
        for k in pair:
            landed(blocks.at[:, :, (place + depth - k) % depth, far_core], x_r.at[k])

    @pl.loop(0, slots, step=2)
    def _(first):
        both = [first, first + 1]
        for j in both:
            landed(stat.at[j], load_o.at[j])

        def statistics(dims):
            for j in both:
                g = blocks[j].reshape(block, block)
                stat[j] = DECAY_RATE * stat[j] + dot(g, g, dims)
                pltpu.make_async_copy(stat.at[j], new.at[0, j], save_n.at[j]).start()

        pl.when(core == 0)(lambda: statistics(((1,), (1,))))
        pl.when(core == 1)(lambda: statistics(((0,), (0,))))

        def each(f, *lists):
            return [f(*values) for values in zip(*lists)]

        a = [stat[j] for j in both]
        norm2 = each(
            lambda a: jnp.sum(jnp.sum(a * a, axis=0, keepdims=True), axis=1, keepdims=True) + EPSILON, a
        )
        norm = each(jnp.sqrt, norm2)
        inverse = each(lambda n: 1.0 / n, norm)
        b1 = each(lambda a, v: (a * v).astype(BF16), a, inverse)
        m2 = each(dot, b1, b1)
        b2 = each(lambda m: m.astype(BF16), m2)
        m3 = each(dot, b1, b2)
        b3 = each(lambda m: m.astype(BF16), m3)
        c4, c5, c6 = (jnp.asarray(v, BF16) for v in COEF[4:])
        upper = each(lambda x, y, w: c4 * x + c5 * y + c6 * w, b1, b2, b3)
        high = each(dot, b3, upper)
        low = each(
            lambda a, v, m2, m3: (COEF[1] * v) * a + COEF[2] * m2 + COEF[3] * m3 + eye[...],
            a, inverse, m2, m3,
        )
        x = each(lambda h, l, n: ((h + l) * lax.rsqrt(jnp.sqrt(n))).astype(BF16), high, low, norm)
        for j, value in zip(both, x):
            root[j] = value.reshape(root.shape[1:])
            remote(root.at[j], other.at[j], root_s.at[j], root_r.at[j], partner).start()

    def apply(j, left, right):
        g = blocks[j].reshape(block, block)
        part = dot(g, right[j].reshape(block, block)).astype(BF16)
        rows = left[j, :, :, core].reshape(block // 2, block)
        return dot(rows, part).astype(BF16)

    matrix_id = lax.broadcasted_iota(jnp.int32, sums.shape[1:], 0)

    @pl.loop(0, slots)
    def _(j):
        landed(other.at[j], root_r.at[j])

        @pl.when(core == 0)
        def _():
            half_out[j] = apply(j, root, other).reshape(half_out.shape[1:])

        @pl.when(core == 1)
        def _():
            half_out[j] = apply(j, other, root).reshape(half_out.shape[1:])

        value = half_out[j].reshape(block // 2, block).astype(F32)
        total = fold(value * value)
        sums[1] = sums[1] + jnp.where(matrix_id == tab[p.matrix_row + j, me], total, 0.0)

    sums_z[place] = sums[...]

    @pl.loop(1, depth)
    def _(step):
        remote(sums, sums_z.at[place], qz_s, qz_r, at(line, (place + step) % depth)).start()

    for pair in p.back_steps:
        for k in pair:
            if k:
                to = (place + depth - k) % depth
                remote(half_out.at[:, :, to], land_c[k - 1], c_s.at[k], c_r.at[k], at(line, to)).start()

    def back_across(a, pair):
        for k in pair:
            if k:
                landed(land_c[k - 1], c_r.at[k])

        @pl.loop(0, lines)
        def _(to):
            for i, k in enumerate(pair):
                slot = tab[SLOT_ROW + to // tall, line * depth + (place + k) % depth]
                if k:
                    send_d[a][to, i] = land_c[k - 1][slot, to % tall]
                else:
                    send_d[a][to, i] = half_out[slot, to % tall, place]

        spot = pl.ds(p.start[a] + line * len(pair), len(pair))

        @pl.loop(1, lines)
        def _(step):
            to = (line + step) % lines
            remote(send_d[a].at[to], land_d.at[core, spot], d_s.at[a], d_r.at[a], at(to, place)).start()

        land_d[core, spot] = send_d[a][line]

    def back_pair(a, pair):
        landed(land_d.at[core, pl.ds(0, (lines - 1) * len(pair))], d_r.at[a])
        rows = land_d.at[core, pl.ds(p.start[a], lines * len(pair))]
        remote(rows, rows, y_s.at[a], y_r.at[a], partner).start()

    for a in range(p.pairs + AHEAD):
        if a < p.pairs:
            back_across(a, p.back_steps[a])
        if a == 1:
            landed(sums_z.at[pl.ds(0, depth - 1)], qz_r)
            sums_l[line] = jnp.sum(sums_z[...], axis=0)

            @pl.loop(1, lines)
            def _(step):
                remote(sums_l.at[line], sums_l.at[line], ql_s, ql_r, at((line + step) % lines, place)).start()

        if a == p.pairs - 1:
            landed(sums_l.at[pl.ds(0, lines - 1)], ql_r)
            sums_c[0] = jnp.sum(sums_l[...], axis=0)
            remote(sums_c.at[0], sums_c.at[1], qc_s, qc_r, partner).start()
        if a >= AHEAD:
            back_pair(a - AHEAD, p.back_steps[a - AHEAD])

    landed(sums_c.at[1], qc_r)
    total = jnp.sum(sums_c[0] + sums_c[1], axis=2, keepdims=True)
    count = float(p.slab * p.fsdp * p.model)
    scale = jnp.sqrt((total[0] / count + EPSILON) / (total[1] / count + EPSILON))
    wide[...] = jnp.broadcast_to(scale, wide.shape)
    for a, pair in enumerate(p.back_steps):
        landed(land_d.at[far_core, pl.ds(p.start[a], lines * len(pair))], y_r.at[a])

    @pl.loop(0, p.matrices)
    def _(m):
        factor = wide[pl.ds(m, 1), :]
        for c in range(columns):
            spot = tab[p.land_row + m * columns + c, 0]
            for h in range(2):
                piece = land_d[h, spot].astype(F32) * factor
                made[m, h * half : (h + 1) * half, c * block : (c + 1) * block] = piece.astype(BF16)
        pltpu.make_async_copy(made.at[m], upd.at[m], save_u.at[m]).start()

    for i in range(parts):
        landed(theirs.at[pl.ds(i * per, per)], pair_s.at[i])
    for a, pair in enumerate(p.back_steps):
        landed(send_a[a].at[pl.ds(0, lines - 1)], a_s.at[a])
        landed(send_d[a].at[pl.ds(0, lines - 1)], d_s.at[a])
        landed(land_d.at[core, pl.ds(p.start[a], lines * len(pair))], y_s.at[a])
    for k in range(depth):
        landed(blocks.at[:, :, (place + depth - k) % depth, core], x_s.at[k])
        if k:
            landed(send_b.at[k - 1], b_s.at[k])
            landed(land_c[k - 1], c_s.at[k])
    for j in range(slots):
        landed(root.at[j], root_s.at[j])
        landed(stat.at[j], save_n.at[j])
    landed(sums_z.at[pl.ds(0, depth - 1)], qz_s)
    landed(sums_l.at[pl.ds(0, lines - 1)], ql_s)
    landed(sums_c.at[0], qc_s)
    for m in range(p.matrices):
        landed(made.at[m], save_u.at[m])


def tables(p, owner, me, line, place):
    groups, columns, lines, depth = p.groups, p.columns, p.lines, p.depth

    def bits(n):
        assert n & (n - 1) == 0
        return n.bit_length() - 1

    group = lax.shift_right_logical(owner, bits(columns)) & (groups - 1)
    matrix = lax.shift_right_logical(owner, bits(columns * groups))
    local = matrix * columns + (owner & (columns - 1))
    code = jnp.zeros((1, p.fsdp), jnp.int32)
    for j in range(p.slots):
        here = group[j : j + 1] == me // p.span
        code = code + jnp.where(here, local[j : j + 1] + 1, 0)
    group_id = lax.broadcasted_iota(jnp.int32, (groups, p.fsdp), 0)
    slot = jnp.zeros((groups, p.fsdp), jnp.int32)
    for j in range(1, p.slots):
        slot = slot + jnp.where(group[j : j + 1] == group_id, j, 0)
    lane = lax.broadcasted_iota(jnp.int32, (1, p.fsdp), 1)
    gap = ((lane & (depth - 1)) - place) & (depth - 1)
    land = jnp.zeros((1, p.fsdp), jnp.int32)
    for a, pair in enumerate(p.back_steps):
        for i, k in enumerate(pair):
            spot = p.start[a] + lax.shift_right_logical(lane, bits(depth)) * len(pair) + i
            land = land + jnp.where(gap == k, spot, 0)
    block_id = lax.broadcasted_iota(jnp.int32, (p.matrices * columns, p.fsdp), 0)
    hit = jnp.where(code == block_id + 1, land, 0)
    hit = jnp.broadcast_to(jnp.sum(hit, axis=1, keepdims=True), hit.shape)
    return [
        (0, jnp.clip(code - 1, 0, p.matrices * columns - 1)),
        (GROUP_ROW, group),
        (SLOT_ROW, jnp.minimum(slot, p.slots - 1)),
        (p.land_row, jnp.minimum(hit, lines * depth - 1)),
        (p.matrix_row, matrix),
    ]


def store_kernel(upd, new, upd_out, new_out, sems):
    copies = [(upd.at[m], upd_out.at[m]) for m in range(upd.shape[0])]
    copies += [(new.at[0, j], new_out.at[0, j]) for j in range(new.shape[1])]
    copies = [pltpu.make_async_copy(a, b, sems.at[i]) for i, (a, b) in enumerate(copies)]
    for copy in copies:
        copy.start()
    for copy in copies:
        copy.wait()


def body(p, gradient, old_stats, owner_table):
    depth, lines, slots, block = p.depth, p.lines, p.slots, p.block
    half, tall, pairs = p.half, p.tall, p.pairs
    dma = pltpu.SemaphoreType.DMA
    vm = pltpu.VMEM
    full = (slots, tall, depth, 2, half, block)
    scratch = [
        vm((p.matrices, half, p.model), BF16),
        vm((p.matrices, half, p.model), BF16),
        vm((p.matrices * p.columns, half, block), BF16),
        [vm((lines, len(pair), half, block), BF16) for pair in p.out_steps],
        [vm((lines, len(pair), half, block), BF16) for pair in p.out_steps],
        vm((depth - 1, slots, tall, half, block), BF16),
        vm(full, BF16),
        vm((block, block), F32),
        vm(full, BF16),
        vm(full, BF16),
        vm((slots, tall, depth, half, block), BF16),
        [vm((slots, tall, half, block), BF16) for _ in range(depth - 1)],
        [vm((lines, len(pair), half, block), BF16) for pair in p.back_steps],
        vm((2, lines * depth, half, block), BF16),
        vm((2, p.matrices, 128), F32),
        vm((p.matrices, block), F32),
        vm((depth, 2, p.matrices, 128), F32),
        vm((lines, 2, p.matrices, 128), F32),
        vm((2, 2, p.matrices, 128), F32),
        vm((p.table_rows, p.fsdp), jnp.int32),
        pltpu.SMEM((p.table_rows, p.fsdp), jnp.int32),
        vm((slots, block, block), F32),
        vm((p.matrices, p.slab, p.model), BF16),
        vm((slots, p.fsdp), jnp.int32),
    ]
    counts = [4, slots, slots, p.matrices, 4, 4, pairs, pairs, depth, depth]
    counts += [depth, depth, slots, slots, depth, depth, pairs, pairs, pairs, pairs]
    scratch += [dma((count,)) for count in counts]
    scratch += [dma] * 8
    update, fresh = pl.pallas_call(
        functools.partial(kernel, p),
        out_shape=(
            jax.ShapeDtypeStruct((p.matrices, p.slab, p.model), BF16),
            jax.ShapeDtypeStruct(old_stats.shape, F32),
        ),
        in_specs=[
            pl.BlockSpec(memory_space=pltpu.HBM),
            pl.BlockSpec(memory_space=pltpu.HBM),
            pl.BlockSpec(memory_space=pltpu.HBM),
        ],
        out_specs=(pl.BlockSpec(memory_space=pl.ANY), pl.BlockSpec(memory_space=pl.ANY)),
        scratch_shapes=scratch,
        compiler_params=pltpu.CompilerParams(
            collective_id=0, has_side_effects=True, vmem_limit_bytes=VMEM_BYTES
        ),
        name="shampoo",
    )(owner_table.T, gradient, old_stats)
    anywhere = pl.BlockSpec(memory_space=pl.ANY)
    return pl.pallas_call(
        store_kernel,
        out_shape=(
            jax.ShapeDtypeStruct(update.shape, BF16),
            jax.ShapeDtypeStruct(fresh.shape, F32),
        ),
        in_specs=[anywhere, anywhere],
        out_specs=(anywhere, anywhere),
        scratch_shapes=[dma((p.matrices + slots,))],
        name="store",
    )(update, fresh)


def solution(mesh):
    def whole(gradient, old_stats, owner_table):
        fsdp = mesh.shape["fsdp"]
        _, matrices, rows, model = gradient.shape
        p = Plan(fsdp, matrices, rows // fsdp, model, owner_table.shape[1], old_stats.shape[2])
        return jax.shard_map(
            functools.partial(body, p),
            mesh=mesh,
            in_specs=(P("rep", None, "fsdp", None), P("rep", "fsdp", None, None), P()),
            out_specs=(P(None, "fsdp", None), P("rep", "fsdp", None, None)),
            check_vma=False,
        )(gradient, old_stats, owner_table)

    return whole
```

```python
import functools

import jax
import jax.numpy as jnp
from jax import lax
from jax.experimental import pallas as pl
from jax.experimental.pallas import tpu as pltpu
from jax.sharding import PartitionSpec as P

DECAY_RATE = 0.95
EPSILON = 1e-06
MESH = pl.DeviceIdType.MESH
F32 = jnp.float32
BF16 = jnp.bfloat16
VMEM_BYTES = 44 * 1024 * 1024

DEPTH = 8
GROUP_ROW, SLOT_ROW = 8, 16
AHEAD = 2

COEF = tuple(
    v / 4096.0 for v in (6400.0, -4405.0, 3125.0, -1250.0, 250.0, -25.0, 1.0)
)


def steps_of(depth):
    pairs = [[low, depth - low] for low in range(depth // 2 - 1, 0, -1)]
    return [[depth // 2]] + pairs + [[0]]


class Plan:
    def __init__(self, fsdp, matrices, slab, model, slots, block):
        self.fsdp, self.matrices, self.slab, self.model = fsdp, matrices, slab, model
        self.slots, self.block = slots, block
        self.depth = DEPTH
        self.lines = fsdp // self.depth
        self.columns = model // block
        self.span = block // slab
        self.groups = fsdp // self.span
        self.tall = self.span // self.depth
        self.half = slab // 2
        self.out_steps = steps_of(self.depth)
        self.back_steps = [list(reversed(pair)) for pair in reversed(self.out_steps)]
        self.pairs = len(self.out_steps)
        self.land_row = SLOT_ROW + self.groups
        self.matrix_row = self.land_row + matrices * self.columns
        self.table_rows = -(-(self.matrix_row + slots) // 8) * 8
        self.start = [self.lines * sum(map(len, self.back_steps[:a])) for a in range(self.pairs)]


def dot(a, b, dims=((1,), (0,))):
    return lax.dot_general(a, b, (dims, ((), ())), preferred_element_type=F32)


def fold(rows):
    line = jnp.sum(rows, axis=0, keepdims=True)
    total = line[:, :128]
    for at in range(128, line.shape[1], 128):
        total = total + line[:, at : at + 128]
    return total


def kernel(p, owners, grad, old, upd, new, *scratch):
    (mine, theirs, gsum, send_a, land_a, send_b, blocks, eye, root, other, half_out) = scratch[:11]
    (land_c, send_d, land_d, sums, wide, sums_z, sums_l, sums_c, draft, tab, stat, made, listed, whole, land_e) = scratch[11:26]
    (load_g, load_o, save_n, save_u, pair_s, pair_r, a_s, a_r, b_s, b_r) = scratch[26:36]
    (x_s, x_r, root_s, root_r, c_s, c_r, d_s, d_r, y_s, y_r) = scratch[36:46]
    (qz_s, qz_r, ql_s, ql_r, qc_s, qc_r, tab_s, list_s, p_s, p_r) = scratch[46:]

    depth, lines, slots, block = p.depth, p.lines, p.slots, p.block
    half, tall, columns = p.half, p.tall, p.columns
    me = lax.axis_index("fsdp")
    core = lax.axis_index("rep")
    far_core = 1 - core
    line = me // depth
    place = me % depth
    partner = (me, far_core)

    def at(other_line, other_place):
        return (other_line * depth + other_place, core)

    def remote(src, dst, send, recv, device):
        return pltpu.make_async_remote_copy(
            src_ref=src, dst_ref=dst, send_sem=send, recv_sem=recv,
            device_id=device, device_id_type=MESH,
        )

    def landed(ref, sem):
        pltpu.make_async_copy(ref, ref, sem).wait()

    my_rows = pl.ds(pl.multiple_of(core * half, half), half)
    far_rows = pl.ds(pl.multiple_of(far_core * half, half), half)

    barrier = pltpu.get_barrier_semaphore()

    def greet(device):
        pl.semaphore_signal(barrier, inc=1, device_id=device, device_id_type=MESH)

    greet(partner)

    @pl.loop(1, depth)
    def _(step):
        greet(at(line, (place + step) % depth))

    @pl.loop(1, lines)
    def _(step):
        greet(at((line + step) % lines, place))

    listing = pltpu.make_async_copy(owners, listed, list_s)
    listing.start()
    parts = 4
    per = p.matrices // parts
    for i in range(parts):
        m = pl.ds(i * per, per)
        pltpu.make_async_copy(grad.at[0, m, my_rows, :], mine.at[m], load_g.at[i]).start()
    for j in range(slots):
        pltpu.make_async_copy(old.at[0, j], stat.at[j], load_o.at[j]).start()
    sums[...] = jnp.zeros_like(sums)
    listing.wait()
    lookup = tables(p, listed[...], me, line, place)
    for row, value in lookup:
        draft[row : row + value.shape[0], :] = value
    pltpu.make_async_copy(draft, tab, tab_s).start()
    row_id = lax.broadcasted_iota(jnp.int32, (block, block), 0)
    col_id = lax.broadcasted_iota(jnp.int32, (block, block), 1)
    eye[...] = jnp.where(row_id == col_id, COEF[0], 0.0)
    pl.semaphore_wait(barrier, depth + lines - 1)

    for i in range(parts):
        m = pl.ds(i * per, per)
        remote(grad.at[0, m, far_rows, :], theirs.at[m], pair_s.at[i], pair_r.at[i], partner).start()
    for i in range(parts):
        m = pl.ds(i * per, per)
        landed(mine.at[m], load_g.at[i])
        landed(theirs.at[m], pair_r.at[i])

        @pl.loop(i * per, (i + 1) * per)
        def _(m):
            square = jnp.zeros((half, block), F32)
            for c in range(columns):
                cut = slice(c * block, (c + 1) * block)
                value = (mine[m, :, cut].astype(F32) + theirs[m, :, cut].astype(F32)).astype(BF16)
                gsum[m * columns + c] = value
                value = value.astype(F32)
                square = square + value * value
            sums[0, pl.ds(m, 1), :] = fold(square)

    landed(tab, tab_s)

    def across(a, pair):
        @pl.loop(0, lines)
        def _(to):
            for i, k in enumerate(pair):
                piece = gsum[tab[0, to * depth + (place + k) % depth]]
                send_a[a][to, i] = piece

        @pl.loop(1, lines)
        def _(step):
            to = (line + step) % lines
            remote(send_a[a].at[to], land_a[a].at[line], a_s.at[a], a_r.at[a], at(to, place)).start()

        for i in range(len(pair)):
            land_a[a][line, i] = send_a[a][line, i]

    def along(a, pair):
        landed(land_a[a].at[pl.ds(0, lines - 1)], a_r.at[a])
        for i, k in enumerate(pair):
            to = (place + k) % depth
            for j in range(slots):
                group = tab[GROUP_ROW + j, line * depth + to]
                for t in range(tall):
                    piece = land_a[a][group * tall + t, i]
                    if k:
                        send_b[k - 1, j, t] = piece
                    else:
                        blocks[j, t, place, core] = piece
            if k:
                remote(
                    send_b.at[k - 1], blocks.at[:, :, place, core], b_s.at[k], b_r.at[k], at(line, to)
                ).start()

    for a in range(p.pairs + AHEAD):
        if a < p.pairs:
            across(a, p.out_steps[a])
        if a >= AHEAD:
            along(a - AHEAD, p.out_steps[a - AHEAD])

    for pair in p.out_steps:
        for k in pair:
            rows = blocks.at[:, :, (place + depth - k) % depth, core]
            if k:
                landed(rows, b_r.at[k])
            remote(rows, rows, x_s.at[k], x_r.at[k], partner).start()
    for pair in p.out_steps:
        for k in pair:
            landed(blocks.at[:, :, (place + depth - k) % depth, far_core], x_r.at[k])

    share = slots // 2
    assert share == 2

    @pl.loop(0, 2)
    def _(turn):
        first = (turn + far_core) % 2 * share
        both = [first, first + 1]
        for j in both:
            landed(stat.at[j], load_o.at[j])

        def statistics(dims):
            for j in both:
                g = blocks[j].reshape(block, block)
                stat[j] = DECAY_RATE * stat[j] + dot(g, g, dims)
                pltpu.make_async_copy(stat.at[j], new.at[0, j], save_n.at[j]).start()

        pl.when(core == 0)(lambda: statistics(((1,), (1,))))
        pl.when(core == 1)(lambda: statistics(((0,), (0,))))

        def each(f, *lists):
            return [f(*values) for values in zip(*lists)]

        a = [stat[j] for j in both]
        norm2 = each(
            lambda a: jnp.sum(jnp.sum(a * a, axis=0, keepdims=True), axis=1, keepdims=True) + EPSILON, a
        )
        norm = each(jnp.sqrt, norm2)
        inverse = each(lambda n: 1.0 / n, norm)
        b1 = each(lambda a, v: (a * v).astype(BF16), a, inverse)
        m2 = each(dot, b1, b1)
        b2 = each(lambda m: m.astype(BF16), m2)
        m3 = each(dot, b1, b2)
        b3 = each(lambda m: m.astype(BF16), m3)
        c4, c5, c6 = (jnp.asarray(v, BF16) for v in COEF[4:])
        upper = each(lambda x, y, w: c4 * x + c5 * y + c6 * w, b1, b2, b3)
        high = each(dot, b3, upper)
        low = each(
            lambda a, v, m2, m3: (COEF[1] * v) * a + COEF[2] * m2 + COEF[3] * m3 + eye[...],
            a, inverse, m2, m3,
        )
        x = each(lambda h, l, n: ((h + l) * lax.rsqrt(jnp.sqrt(n))).astype(BF16), high, low, norm)
        for j, value in zip(both, x):
            root[j] = value.reshape(root.shape[1:])

        @pl.when(turn == 0)
        def _():
            for i, j in enumerate(both):
                remote(root.at[j], other.at[i], root_s.at[i], root_r.at[i], partner).start()

    def apply(j, left, right):
        g = blocks[j].reshape(block, block)
        part = dot(g, right.reshape(block, block)).astype(BF16)
        return dot(left.reshape(block, block), part).astype(BF16).reshape(whole.shape[1:])

    matrix_id = lax.broadcasted_iota(jnp.int32, sums.shape[1:], 0)
    for i in range(share):
        j = core * share + i
        landed(other.at[i], root_r.at[i])

        @pl.when(core == 0)
        def _():
            whole[i] = apply(j, root[j], other[i])

        @pl.when(core == 1)
        def _():
            whole[i] = apply(j, other[i], root[j])

        remote(whole.at[i, :, :, far_core], half_out.at[j], p_s.at[i], p_r.at[i], partner).start()
        half_out[j] = whole[i, :, :, core]
        value = whole[i].reshape(block, block).astype(F32)
        total = fold(value * value)
        sums[1] = sums[1] + jnp.where(matrix_id == tab[p.matrix_row + j, me], total, 0.0)
    for i in range(share):
        landed(half_out.at[far_core * share + i], p_r.at[i])

    sums_z[place] = sums[...]

    @pl.loop(1, depth)
    def _(step):
        remote(sums, sums_z.at[place], qz_s, qz_r, at(line, (place + step) % depth)).start()

    for pair in p.back_steps:
        for k in pair:
            if k:
                to = (place + depth - k) % depth
                remote(half_out.at[:, :, to], land_c[k - 1], c_s.at[k], c_r.at[k], at(line, to)).start()

    def back_across(a, pair):
        for k in pair:
            if k:
                landed(land_c[k - 1], c_r.at[k])

        @pl.loop(0, lines)
        def _(to):
            for i, k in enumerate(pair):
                slot = tab[SLOT_ROW + to // tall, line * depth + (place + k) % depth]
                if k:
                    send_d[a][to, i] = land_c[k - 1][slot, to % tall]
                else:
                    send_d[a][to, i] = half_out[slot, to % tall, place]

        spot = pl.ds(p.start[a] + line * len(pair), len(pair))

        @pl.loop(1, lines)
        def _(step):
            to = (line + step) % lines
            remote(send_d[a].at[to], land_d.at[spot], d_s.at[a], d_r.at[a], at(to, place)).start()

        land_d[spot] = send_d[a][line]

    def back_pair(a, pair):
        landed(land_d.at[pl.ds(0, (lines - 1) * len(pair))], d_r.at[a])
        rows = pl.ds(p.start[a], lines * len(pair))
        remote(land_d.at[rows], land_e.at[rows], y_s.at[a], y_r.at[a], partner).start()

    for a in range(p.pairs + AHEAD):
        if a < p.pairs:
            back_across(a, p.back_steps[a])
        if a == 1:
            landed(sums_z.at[pl.ds(0, depth - 1)], qz_r)
            sums_l[line] = jnp.sum(sums_z[...], axis=0)

            @pl.loop(1, lines)
            def _(step):
                remote(sums_l.at[line], sums_l.at[line], ql_s, ql_r, at((line + step) % lines, place)).start()

        if a == p.pairs - 1:
            landed(sums_l.at[pl.ds(0, lines - 1)], ql_r)
            sums_c[0] = jnp.sum(sums_l[...], axis=0)
            remote(sums_c.at[0], sums_c.at[1], qc_s, qc_r, partner).start()
        if a >= AHEAD:
            back_pair(a - AHEAD, p.back_steps[a - AHEAD])

    landed(sums_c.at[1], qc_r)
    total = jnp.sum(sums_c[0] + sums_c[1], axis=2, keepdims=True)
    count = float(p.slab * p.fsdp * p.model)
    scale = jnp.sqrt((total[0] / count + EPSILON) / (total[1] / count + EPSILON))
    wide[...] = jnp.broadcast_to(scale, wide.shape)
    def place_rows(source, h, m):
        factor = wide[pl.ds(m, 1), :]
        rows = pl.ds(pl.multiple_of(h * half, half), half)
        for c in range(columns):
            piece = source[tab[p.land_row + m * columns + c, 0]].astype(F32) * factor
            made[m, rows, c * block : (c + 1) * block] = piece.astype(BF16)

    @pl.loop(0, p.matrices)
    def _(m):
        place_rows(land_d, core, m)

    for a, pair in enumerate(p.back_steps):
        landed(land_e.at[pl.ds(p.start[a], lines * len(pair))], y_r.at[a])

    @pl.loop(0, p.matrices)
    def _(m):
        place_rows(land_e, far_core, m)
        pltpu.make_async_copy(made.at[m], upd.at[m], save_u.at[m]).start()

    for i in range(parts):
        landed(theirs.at[pl.ds(i * per, per)], pair_s.at[i])
    for a, pair in enumerate(p.back_steps):
        landed(send_a[a].at[pl.ds(0, lines - 1)], a_s.at[a])
        landed(send_d[a].at[pl.ds(0, lines - 1)], d_s.at[a])
        landed(land_d.at[pl.ds(p.start[a], lines * len(pair))], y_s.at[a])
    for k in range(depth):
        landed(blocks.at[:, :, (place + depth - k) % depth, core], x_s.at[k])
        if k:
            landed(send_b.at[k - 1], b_s.at[k])
            landed(land_c[k - 1], c_s.at[k])
    for j in range(slots):
        landed(stat.at[j], save_n.at[j])
    for i in range(share):
        landed(root.at[i], root_s.at[i])
        landed(whole.at[i, :, :, far_core], p_s.at[i])
    landed(sums_z.at[pl.ds(0, depth - 1)], qz_s)
    landed(sums_l.at[pl.ds(0, lines - 1)], ql_s)
    landed(sums_c.at[0], qc_s)
    for m in range(p.matrices):
        landed(made.at[m], save_u.at[m])


def tables(p, owner, me, line, place):
    groups, columns, lines, depth = p.groups, p.columns, p.lines, p.depth

    def bits(n):
        assert n & (n - 1) == 0
        return n.bit_length() - 1

    group = lax.shift_right_logical(owner, bits(columns)) & (groups - 1)
    matrix = lax.shift_right_logical(owner, bits(columns * groups))
    local = matrix * columns + (owner & (columns - 1))
    code = jnp.zeros((1, p.fsdp), jnp.int32)
    for j in range(p.slots):
        here = group[j : j + 1] == me // p.span
        code = code + jnp.where(here, local[j : j + 1] + 1, 0)
    group_id = lax.broadcasted_iota(jnp.int32, (groups, p.fsdp), 0)
    slot = jnp.zeros((groups, p.fsdp), jnp.int32)
    for j in range(1, p.slots):
        slot = slot + jnp.where(group[j : j + 1] == group_id, j, 0)
    lane = lax.broadcasted_iota(jnp.int32, (1, p.fsdp), 1)
    gap = ((lane & (depth - 1)) - place) & (depth - 1)
    land = jnp.zeros((1, p.fsdp), jnp.int32)
    for a, pair in enumerate(p.back_steps):
        for i, k in enumerate(pair):
            spot = p.start[a] + lax.shift_right_logical(lane, bits(depth)) * len(pair) + i
            land = land + jnp.where(gap == k, spot, 0)
    block_id = lax.broadcasted_iota(jnp.int32, (p.matrices * columns, p.fsdp), 0)
    hit = jnp.where(code == block_id + 1, land, 0)
    hit = jnp.broadcast_to(jnp.sum(hit, axis=1, keepdims=True), hit.shape)
    return [
        (0, jnp.clip(code - 1, 0, p.matrices * columns - 1)),
        (GROUP_ROW, group),
        (SLOT_ROW, jnp.minimum(slot, p.slots - 1)),
        (p.land_row, jnp.minimum(hit, lines * depth - 1)),
        (p.matrix_row, matrix),
    ]


def body(p, gradient, old_stats, owner_table):
    depth, lines, slots, block = p.depth, p.lines, p.slots, p.block
    half, tall, pairs = p.half, p.tall, p.pairs
    dma = pltpu.SemaphoreType.DMA
    vm = pltpu.VMEM
    full = (slots, tall, depth, 2, half, block)
    scratch = [
        vm((p.matrices, half, p.model), BF16),
        vm((p.matrices, half, p.model), BF16),
        vm((p.matrices * p.columns, half, block), BF16),
        [vm((lines, len(pair), half, block), BF16) for pair in p.out_steps],
        [vm((lines, len(pair), half, block), BF16) for pair in p.out_steps],
        vm((depth - 1, slots, tall, half, block), BF16),
        vm(full, BF16),
        vm((block, block), F32),
        vm(full, BF16),
        vm((2,) + full[1:], BF16),
        vm((slots, tall, depth, half, block), BF16),
        [vm((slots, tall, half, block), BF16) for _ in range(depth - 1)],
        [vm((lines, len(pair), half, block), BF16) for pair in p.back_steps],
        vm((lines * depth, half, block), BF16),
        vm((2, p.matrices, 128), F32),
        vm((p.matrices, block), F32),
        vm((depth, 2, p.matrices, 128), F32),
        vm((lines, 2, p.matrices, 128), F32),
        vm((2, 2, p.matrices, 128), F32),
        vm((p.table_rows, p.fsdp), jnp.int32),
        pltpu.SMEM((p.table_rows, p.fsdp), jnp.int32),
        vm((slots, block, block), F32),
        vm((p.matrices, p.slab, p.model), BF16),
        vm((slots, p.fsdp), jnp.int32),
        vm((2,) + full[1:], BF16),
        vm((lines * depth, half, block), BF16),
    ]
    counts = [4, slots, slots, p.matrices, 4, 4, pairs, pairs, depth, depth]
    counts += [depth, depth, 2, 2, depth, depth, pairs, pairs, pairs, pairs]
    scratch += [dma((count,)) for count in counts]
    scratch += [dma] * 8 + [dma((2,))] * 2
    update, fresh = pl.pallas_call(
        functools.partial(kernel, p),
        out_shape=(
            jax.ShapeDtypeStruct((p.matrices, p.slab, p.model), BF16),
            jax.ShapeDtypeStruct(old_stats.shape, F32),
        ),
        in_specs=[
            pl.BlockSpec(memory_space=pltpu.HBM),
            pl.BlockSpec(memory_space=pltpu.HBM),
            pl.BlockSpec(memory_space=pltpu.HBM),
        ],
        out_specs=(pl.BlockSpec(memory_space=pl.ANY), pl.BlockSpec(memory_space=pl.ANY)),
        scratch_shapes=scratch,
        compiler_params=pltpu.CompilerParams(
            collective_id=0, has_side_effects=True, vmem_limit_bytes=VMEM_BYTES
        ),
        name="shampoo",
    )(owner_table.T, gradient, old_stats)
    return update, fresh


def solution(mesh):
    def whole(gradient, old_stats, owner_table):
        fsdp = mesh.shape["fsdp"]
        _, matrices, rows, model = gradient.shape
        p = Plan(fsdp, matrices, rows // fsdp, model, owner_table.shape[1], old_stats.shape[2])
        return jax.shard_map(
            functools.partial(body, p),
            mesh=mesh,
            in_specs=(P("rep", None, "fsdp", None), P("rep", "fsdp", None, None), P()),
            out_specs=(P(None, "fsdp", None), P("rep", "fsdp", None, None)),
            check_vma=False,
        )(gradient, old_stats, owner_table)

    return whole
```

```python
import functools

import jax
import jax.numpy as jnp
from jax import lax
from jax.experimental import pallas as pl
from jax.experimental.pallas import tpu as pltpu
from jax.sharding import PartitionSpec as P

DECAY_RATE = 0.95
EPSILON = 1e-06
MESH = pl.DeviceIdType.MESH
F32 = jnp.float32
BF16 = jnp.bfloat16
VMEM_BYTES = 44 * 1024 * 1024

DEPTH = 8
GROUP_ROW, SLOT_ROW = 8, 16
AHEAD = 3
SPLIT = 2

COEF = tuple(
    v / 4096.0 for v in (6400.0, -4405.0, 3125.0, -1250.0, 250.0, -25.0, 1.0)
)


def steps_of(depth):
    pairs = [[low, depth - low] for low in range(depth // 2 - 1, 0, -1)]
    return [[depth // 2]] + pairs + [[0]]


class Plan:
    def __init__(self, fsdp, matrices, slab, model, slots, block):
        self.fsdp, self.matrices, self.slab, self.model = fsdp, matrices, slab, model
        self.slots, self.block = slots, block
        self.depth = DEPTH
        self.lines = fsdp // self.depth
        self.columns = model // block
        self.span = block // slab
        self.groups = fsdp // self.span
        self.tall = self.span // self.depth
        self.half = slab // 2
        self.out_steps = steps_of(self.depth)
        self.back_steps = [list(reversed(pair)) for pair in reversed(self.out_steps)]
        self.pairs = len(self.out_steps)
        self.wide = block // SPLIT
        self.land_row = SLOT_ROW + self.groups
        self.matrix_row = self.land_row + matrices * self.columns
        self.table_rows = -(-(self.matrix_row + slots) // 8) * 8
        self.start = [self.lines * sum(map(len, self.back_steps[:a])) for a in range(self.pairs)]


def dot(a, b, dims=((1,), (0,))):
    return lax.dot_general(a, b, (dims, ((), ())), preferred_element_type=F32)


def fold(rows):
    line = jnp.sum(rows, axis=0, keepdims=True)
    total = line[:, :128]
    for at in range(128, line.shape[1], 128):
        total = total + line[:, at : at + 128]
    return total


def kernel(p, owners, grad, old, upd, new, *scratch):
    (mine, theirs, gsum, send_a, land_a, send_b, blocks, eye, root, other, half_out) = scratch[:11]
    (land_c, send_d, land_d, sums, scales, sums_z, sums_l, sums_c, draft, tab, stat, made, listed, whole, land_e) = scratch[11:26]
    (load_g, load_o, save_n, save_u, pair_s, pair_r, a_s, a_r, b_s, b_r) = scratch[26:36]
    (x_s, x_r, root_s, root_r, c_s, c_r, d_s, d_r, y_s, y_r) = scratch[36:46]
    (qz_s, qz_r, ql_s, ql_r, qc_s, qc_r, tab_s, list_s, p_s, p_r) = scratch[46:]

    depth, lines, slots, block = p.depth, p.lines, p.slots, p.block
    half, tall, columns, wide, pairs = p.half, p.tall, p.columns, p.wide, p.pairs
    me = lax.axis_index("fsdp")
    core = lax.axis_index("rep")
    far_core = 1 - core
    line = lax.div(me, depth)
    place = lax.rem(me, depth)
    ahead = [lax.rem(place + k, depth) for k in range(depth)]
    behind = [lax.rem(place + depth - k, depth) for k in range(depth)]
    partner = (me, far_core)

    def at(other_line, other_place):
        return (other_line * depth + other_place, core)

    def remote(src, dst, send, recv, device):
        return pltpu.make_async_remote_copy(
            src_ref=src, dst_ref=dst, send_sem=send, recv_sem=recv,
            device_id=device, device_id_type=MESH,
        )

    def landed(ref, sem):
        pltpu.make_async_copy(ref, ref, sem).wait()

    my_rows = pl.ds(pl.multiple_of(core * half, half), half)
    far_rows = pl.ds(pl.multiple_of(far_core * half, half), half)

    barrier = pltpu.get_barrier_semaphore()

    def greet(device):
        pl.semaphore_signal(barrier, inc=1, device_id=device, device_id_type=MESH)

    greet(partner)

    @pl.loop(1, depth)
    def _(step):
        greet(at(line, lax.rem(place + step, depth)))

    @pl.loop(1, lines)
    def _(step):
        greet(at(lax.rem(line + step, lines), place))

    listing = pltpu.make_async_copy(owners, listed, list_s)
    listing.start()
    part_of = p.matrices // SPLIT

    def cut(q, c=0):
        return pl.ds(c * block + q * wide, wide)

    for q in range(SPLIT):
        for c in range(columns):
            pltpu.make_async_copy(
                grad.at[0, :, my_rows, cut(q, c)], mine.at[:, :, cut(q, c)], load_g.at[q]
            ).start()
    for j in range(slots):
        pltpu.make_async_copy(old.at[0, j], stat.at[j], load_o.at[j]).start()
    sums[...] = jnp.zeros_like(sums)
    listing.wait()
    lookup = tables(p, listed[...], me, line, place)
    for row, value in lookup:
        draft[row : row + value.shape[0], :] = value
    pltpu.make_async_copy(draft, tab, tab_s).start()
    row_id = lax.broadcasted_iota(jnp.int32, (block, block), 0)
    col_id = lax.broadcasted_iota(jnp.int32, (block, block), 1)
    eye[...] = jnp.where(row_id == col_id, COEF[0], 0.0)
    pl.semaphore_wait(barrier, depth + lines - 1)

    for q in range(SPLIT):
        for c in range(columns):
            remote(
                grad.at[0, :, far_rows, cut(q, c)], theirs.at[:, :, cut(q, c)],
                pair_s.at[q], pair_r.at[q], partner,
            ).start()

    def add(q):
        landed(mine.at[pl.ds(0, part_of)], load_g.at[q])
        landed(theirs.at[pl.ds(0, part_of)], pair_r.at[q])

        @pl.loop(0, p.matrices)
        def _(m):
            square = jnp.zeros((half, wide), F32)
            for c in range(columns):
                value = mine[m, :, cut(q, c)].astype(F32) + theirs[m, :, cut(q, c)].astype(F32)
                value = value.astype(BF16)
                gsum[q][m * columns + c] = value
                value = value.astype(F32)
                square = square + value * value
            sums[0, pl.ds(m, 1), :] = sums[0, pl.ds(m, 1), :] + fold(square)

    add(0)
    landed(tab, tab_s)

    def across(q, a, pair):
        @pl.loop(0, lines, unroll=4)
        def _(to):
            for i, k in enumerate(pair):
                send_a[q][a][to, i] = gsum[q][tab[0, to * depth + ahead[k]]]

        @pl.loop(1, lines, unroll=5)
        def _(step):
            to = lax.rem(line + step, lines)
            remote(
                send_a[q][a].at[to], land_a[q][a].at[line],
                a_s.at[q * pairs + a], a_r.at[q * pairs + a], at(to, place),
            ).start()

        for i in range(len(pair)):
            land_a[q][a][line, i] = send_a[q][a][line, i]

    def along(q, a, pair):
        landed(land_a[q][a].at[pl.ds(0, lines - 1)], a_r.at[q * pairs + a])
        for i, k in enumerate(pair):
            to = ahead[k]
            for j in range(slots):
                group = tab[GROUP_ROW + j, line * depth + to]
                for t in range(tall):
                    piece = land_a[q][a][group * tall + t, i]
                    if k:
                        send_b[q, k - 1, j, t] = piece
                    else:
                        blocks[j, t, place, core, :, cut(q)] = piece
            if k:
                remote(
                    send_b.at[q, k - 1], blocks.at[:, :, place, core, :, cut(q)],
                    b_s.at[q * depth + k], b_r.at[q * depth + k], at(line, to),
                ).start()

    out_order = [(q, a, pair) for q in range(SPLIT) for a, pair in enumerate(p.out_steps)]
    for at_step in range(len(out_order) + AHEAD):
        if at_step % pairs == min(2, pairs - 1) and at_step // pairs + 1 < SPLIT:
            add(at_step // pairs + 1)
        if at_step < len(out_order):
            across(*out_order[at_step])
        if at_step >= AHEAD:
            along(*out_order[at_step - AHEAD])

    for q, _, pair in out_order:
        for k in pair:
            rows = blocks.at[:, :, behind[k], core, :, cut(q)]
            sem = q * depth + k
            if k:
                landed(rows, b_r.at[sem])
            remote(rows, rows, x_s.at[sem], x_r.at[sem], partner).start()
    for q, _, pair in out_order:
        for k in pair:
            landed(blocks.at[:, :, behind[k], far_core, :, cut(q)], x_r.at[q * depth + k])

    share = slots // 2
    assert share == 2

    @pl.loop(0, 2)
    def _(turn):
        first = lax.rem(turn + far_core, 2) * share
        both = [first, first + 1]
        for j in both:
            landed(stat.at[j], load_o.at[j])

        def statistics(dims):
            for j in both:
                g = blocks[j].reshape(block, block)
                stat[j] = DECAY_RATE * stat[j] + dot(g, g, dims)
                pltpu.make_async_copy(stat.at[j], new.at[0, j], save_n.at[j]).start()

        pl.when(core == 0)(lambda: statistics(((1,), (1,))))
        pl.when(core == 1)(lambda: statistics(((0,), (0,))))

        def each(f, *lists):
            return [f(*values) for values in zip(*lists)]

        a = [stat[j] for j in both]
        norm2 = each(
            lambda a: jnp.sum(jnp.sum(a * a, axis=0, keepdims=True), axis=1, keepdims=True) + EPSILON, a
        )
        norm = each(jnp.sqrt, norm2)
        inverse = each(lambda n: 1.0 / n, norm)
        b1 = each(lambda a, v: (a * v).astype(BF16), a, inverse)
        m2 = each(dot, b1, b1)
        b2 = each(lambda m: m.astype(BF16), m2)
        m3 = each(dot, b1, b2)
        b3 = each(lambda m: m.astype(BF16), m3)
        c4, c5, c6 = (jnp.asarray(v, BF16) for v in COEF[4:])
        upper = each(lambda x, y, w: c4 * x + c5 * y + c6 * w, b1, b2, b3)
        high = each(dot, b3, upper)
        low = each(
            lambda a, v, m2, m3: (COEF[1] * v) * a + COEF[2] * m2 + COEF[3] * m3 + eye[...],
            a, inverse, m2, m3,
        )
        x = each(lambda h, l, n: ((h + l) * lax.rsqrt(jnp.sqrt(n))).astype(BF16), high, low, norm)
        for j, value in zip(both, x):
            root[j] = value.reshape(root.shape[1:])

        @pl.when(turn == 0)
        def _():
            for i, j in enumerate(both):
                remote(root.at[j], other.at[i], root_s.at[i], root_r.at[i], partner).start()

    def apply(j, left, right):
        g = blocks[j].reshape(block, block)
        part = dot(g, right.reshape(block, block)).astype(BF16)
        return dot(left.reshape(block, block), part).astype(BF16).reshape(whole.shape[1:])

    matrix_id = lax.broadcasted_iota(jnp.int32, sums.shape[1:], 0)
    for i in range(share):
        j = core * share + i
        landed(other.at[i], root_r.at[i])

        @pl.when(core == 0)
        def _():
            whole[i] = apply(j, root[j], other[i])

        @pl.when(core == 1)
        def _():
            whole[i] = apply(j, other[i], root[j])

        remote(whole.at[i, :, :, far_core], half_out.at[j], p_s.at[i], p_r.at[i], partner).start()
        half_out[j] = whole[i, :, :, core]
        value = whole[i].reshape(block, block).astype(F32)
        total = fold(value * value)
        sums[1] = sums[1] + jnp.where(matrix_id == tab[p.matrix_row + j, me], total, 0.0)
    for i in range(share):
        landed(half_out.at[far_core * share + i], p_r.at[i])

    sums_z[place] = sums[...]

    @pl.loop(1, depth)
    def _(step):
        remote(sums, sums_z.at[place], qz_s, qz_r, at(line, lax.rem(place + step, depth))).start()

    back_order = [(q, a, pair) for q in range(SPLIT) for a, pair in enumerate(p.back_steps)]
    for q, _, pair in back_order:
        for k in pair:
            if k:
                to, sem = behind[k], q * depth + k
                remote(
                    half_out.at[:, :, to, :, cut(q)], land_c[q][k - 1], c_s.at[sem], c_r.at[sem], at(line, to)
                ).start()

    def back_across(q, a, pair):
        for k in pair:
            if k:
                landed(land_c[q][k - 1], c_r.at[q * depth + k])

        @pl.loop(0, lines, unroll=4)
        def _(to):
            for i, k in enumerate(pair):
                slot = tab[SLOT_ROW + lax.div(to, tall), line * depth + ahead[k]]
                if k:
                    send_d[q][a][to, i] = land_c[q][k - 1][slot, lax.rem(to, tall)]
                else:
                    send_d[q][a][to, i] = half_out[slot, lax.rem(to, tall), place, :, cut(q)]

        spot = pl.ds(p.start[a] + line * len(pair), len(pair))

        @pl.loop(1, lines, unroll=5)
        def _(step):
            to = lax.rem(line + step, lines)
            remote(
                send_d[q][a].at[to], land_d[q].at[spot],
                d_s.at[q * pairs + a], d_r.at[q * pairs + a], at(to, place),
            ).start()

        land_d[q][spot] = send_d[q][a][line]

    def back_pair(q, a, pair):
        sem = q * pairs + a
        landed(land_d[q].at[pl.ds(0, (lines - 1) * len(pair))], d_r.at[sem])
        rows = pl.ds(p.start[a], lines * len(pair))
        remote(land_d[q].at[rows], land_e[q].at[rows], y_s.at[sem], y_r.at[sem], partner).start()

    def far_landed(q):
        for a, pair in enumerate(p.back_steps):
            rows = pl.ds(p.start[a], lines * len(pair))
            landed(land_e[q].at[rows], y_r.at[q * pairs + a])

    def place_rows(q, h, source, m):
        factor = scales[pl.ds(m, 1), :]
        rows = pl.ds(pl.multiple_of(h * half, half), half)
        for c in range(columns):
            piece = source[q][tab[p.land_row + m * columns + c, 0]].astype(F32) * factor
            made[m, rows, cut(q, c)] = piece.astype(BF16)

    def place_both(q):
        far_landed(q)

        @pl.loop(0, p.matrices)
        def _(m):
            place_rows(q, core, land_d, m)
            place_rows(q, far_core, land_e, m)

    def find_scales():
        landed(sums_c.at[1], qc_r)
        total = jnp.sum(sums_c[0] + sums_c[1], axis=2, keepdims=True)
        count = float(p.slab * p.fsdp * p.model)
        scale = jnp.sqrt((total[0] / count + EPSILON) / (total[1] / count + EPSILON))
        scales[...] = jnp.broadcast_to(scale, scales.shape)

    for a in range(len(back_order) + AHEAD):
        if a < len(back_order):
            back_across(*back_order[a])
        if a == 1:
            landed(sums_z.at[pl.ds(0, depth - 1)], qz_r)
            sums_l[line] = jnp.sum(sums_z[...], axis=0)

            @pl.loop(1, lines)
            def _(step):
                remote(sums_l.at[line], sums_l.at[line], ql_s, ql_r, at(lax.rem(line + step, lines), place)).start()

        if a == pairs - 1:
            landed(sums_l.at[pl.ds(0, lines - 1)], ql_r)
            sums_c[0] = jnp.sum(sums_l[...], axis=0)
            remote(sums_c.at[0], sums_c.at[1], qc_s, qc_r, partner).start()
        if a == len(back_order):
            find_scales()
            for q in range(SPLIT - 1):
                place_both(q)
        if a >= AHEAD:
            back_pair(*back_order[a - AHEAD])

    last = SPLIT - 1

    @pl.loop(0, p.matrices)
    def _(m):
        place_rows(last, core, land_d, m)

    far_landed(last)

    @pl.loop(0, p.matrices)
    def _(m):
        place_rows(last, far_core, land_e, m)
        pltpu.make_async_copy(made.at[m], upd.at[m], save_u.at[m]).start()

    for q in range(SPLIT):
        landed(theirs.at[pl.ds(0, part_of)], pair_s.at[q])
        for a, pair in enumerate(p.out_steps):
            landed(send_a[q][a].at[pl.ds(0, lines - 1)], a_s.at[q * pairs + a])
        for a, pair in enumerate(p.back_steps):
            landed(send_d[q][a].at[pl.ds(0, lines - 1)], d_s.at[q * pairs + a])
            landed(land_d[q].at[pl.ds(p.start[a], lines * len(pair))], y_s.at[q * pairs + a])
        for k in range(depth):
            landed(blocks.at[:, :, behind[k], core, :, cut(q)], x_s.at[q * depth + k])
            if k:
                landed(send_b.at[q, k - 1], b_s.at[q * depth + k])
                landed(land_c[q][k - 1], c_s.at[q * depth + k])
    for j in range(slots):
        landed(stat.at[j], save_n.at[j])
    for i in range(share):
        landed(root.at[i], root_s.at[i])
        landed(whole.at[i, :, :, far_core], p_s.at[i])
    landed(sums_z.at[pl.ds(0, depth - 1)], qz_s)
    landed(sums_l.at[pl.ds(0, lines - 1)], ql_s)
    landed(sums_c.at[0], qc_s)
    for m in range(p.matrices):
        landed(made.at[m], save_u.at[m])


def tables(p, owner, me, line, place):
    groups, columns, lines, depth = p.groups, p.columns, p.lines, p.depth

    def bits(n):
        assert n & (n - 1) == 0
        return n.bit_length() - 1

    group = lax.shift_right_logical(owner, bits(columns)) & (groups - 1)
    matrix = lax.shift_right_logical(owner, bits(columns * groups))
    local = matrix * columns + (owner & (columns - 1))
    code = jnp.zeros((1, p.fsdp), jnp.int32)
    for j in range(p.slots):
        here = group[j : j + 1] == lax.div(me, p.span)
        code = code + jnp.where(here, local[j : j + 1] + 1, 0)
    group_id = lax.broadcasted_iota(jnp.int32, (groups, p.fsdp), 0)
    slot = jnp.zeros((groups, p.fsdp), jnp.int32)
    for j in range(1, p.slots):
        slot = slot + jnp.where(group[j : j + 1] == group_id, j, 0)
    lane = lax.broadcasted_iota(jnp.int32, (1, p.fsdp), 1)
    gap = ((lane & (depth - 1)) - place) & (depth - 1)
    land = jnp.zeros((1, p.fsdp), jnp.int32)
    for a, pair in enumerate(p.back_steps):
        for i, k in enumerate(pair):
            spot = p.start[a] + lax.shift_right_logical(lane, bits(depth)) * len(pair) + i
            land = land + jnp.where(gap == k, spot, 0)
    block_id = lax.broadcasted_iota(jnp.int32, (p.matrices * columns, p.fsdp), 0)
    hit = jnp.where(code == block_id + 1, land, 0)
    hit = jnp.broadcast_to(jnp.sum(hit, axis=1, keepdims=True), hit.shape)
    return [
        (0, jnp.clip(code - 1, 0, p.matrices * columns - 1)),
        (GROUP_ROW, group),
        (SLOT_ROW, jnp.minimum(slot, p.slots - 1)),
        (p.land_row, jnp.minimum(hit, lines * depth - 1)),
        (p.matrix_row, matrix),
    ]


def body(p, gradient, old_stats, owner_table):
    depth, lines, slots, block = p.depth, p.lines, p.slots, p.block
    half, tall, wide = p.half, p.tall, p.wide
    pairs, steps = SPLIT * p.pairs, SPLIT * depth
    dma = pltpu.SemaphoreType.DMA
    vm = pltpu.VMEM
    full = (slots, tall, depth, 2, half, block)

    def chunks(order):
        return [[vm((lines, len(pair), half, wide), BF16) for pair in order] for _ in range(SPLIT)]

    scratch = [
        vm((p.matrices, half, p.model), BF16),
        vm((p.matrices, half, p.model), BF16),
        [vm((p.matrices * p.columns, half, wide), BF16) for _ in range(SPLIT)],
        chunks(p.out_steps),
        chunks(p.out_steps),
        vm((SPLIT, depth - 1, slots, tall, half, wide), BF16),
        vm(full, BF16),
        vm((block, block), F32),
        vm(full, BF16),
        vm((2,) + full[1:], BF16),
        vm((slots, tall, depth, half, block), BF16),
        [[vm((slots, tall, half, wide), BF16) for _ in range(depth - 1)] for _ in range(SPLIT)],
        chunks(p.back_steps),
        [vm((lines * depth, half, wide), BF16) for _ in range(SPLIT)],
        vm((2, p.matrices, 128), F32),
        vm((p.matrices, wide), F32),
        vm((depth, 2, p.matrices, 128), F32),
        vm((lines, 2, p.matrices, 128), F32),
        vm((2, 2, p.matrices, 128), F32),
        vm((p.table_rows, p.fsdp), jnp.int32),
        pltpu.SMEM((p.table_rows, p.fsdp), jnp.int32),
        vm((slots, block, block), F32),
        vm((p.matrices, p.slab, p.model), BF16),
        vm((slots, p.fsdp), jnp.int32),
        vm((2,) + full[1:], BF16),
        [vm((lines * depth, half, wide), BF16) for _ in range(SPLIT)],
    ]
    counts = [SPLIT, slots, slots, p.matrices, SPLIT, SPLIT, pairs, pairs, steps, steps]
    counts += [steps, steps, 2, 2, steps, steps, pairs, pairs, pairs, pairs]
    scratch += [dma((count,)) for count in counts]
    scratch += [dma] * 8 + [dma((2,))] * 2
    update, fresh = pl.pallas_call(
        functools.partial(kernel, p),
        out_shape=(
            jax.ShapeDtypeStruct((p.matrices, p.slab, p.model), BF16),
            jax.ShapeDtypeStruct(old_stats.shape, F32),
        ),
        in_specs=[
            pl.BlockSpec(memory_space=pltpu.HBM),
            pl.BlockSpec(memory_space=pltpu.HBM),
            pl.BlockSpec(memory_space=pltpu.HBM),
        ],
        out_specs=(pl.BlockSpec(memory_space=pl.ANY), pl.BlockSpec(memory_space=pl.ANY)),
        scratch_shapes=scratch,
        compiler_params=pltpu.CompilerParams(
            collective_id=0, has_side_effects=True, vmem_limit_bytes=VMEM_BYTES
        ),
        name="shampoo",
    )(owner_table.T, gradient, old_stats)
    return update, fresh


def solution(mesh):
    def whole(gradient, old_stats, owner_table):
        fsdp = mesh.shape["fsdp"]
        _, matrices, rows, model = gradient.shape
        p = Plan(fsdp, matrices, rows // fsdp, model, owner_table.shape[1], old_stats.shape[2])
        return jax.shard_map(
            functools.partial(body, p),
            mesh=mesh,
            in_specs=(P("rep", None, "fsdp", None), P("rep", "fsdp", None, None), P()),
            out_specs=(P(None, "fsdp", None), P("rep", "fsdp", None, None)),
            check_vma=False,
        )(gradient, old_stats, owner_table)

    return whole
```

```python
import functools

import jax
import jax.numpy as jnp
from jax import lax
from jax.experimental import pallas as pl
from jax.experimental.pallas import tpu as pltpu
from jax.sharding import PartitionSpec as P

DECAY_RATE = 0.95
EPSILON = 1e-06
MESH = pl.DeviceIdType.MESH
F32 = jnp.float32
BF16 = jnp.bfloat16
VMEM_BYTES = 44 * 1024 * 1024

DEPTH = 8
GROUP_ROW, SLOT_ROW = 8, 16
AHEAD = 3
SPLIT = 2

COEF = tuple(
    v / 4096.0 for v in (6400.0, -4405.0, 3125.0, -1250.0, 250.0, -25.0, 1.0)
)


def steps_of(depth):
    pairs = [[low, depth - low] for low in range(depth // 2 - 1, 0, -1)]
    return [[depth // 2]] + pairs + [[0]]


class Plan:
    def __init__(self, fsdp, matrices, slab, model, slots, block):
        self.fsdp, self.matrices, self.slab, self.model = fsdp, matrices, slab, model
        self.slots, self.block = slots, block
        self.depth = DEPTH
        self.lines = fsdp // self.depth
        self.columns = model // block
        self.span = block // slab
        self.groups = fsdp // self.span
        self.tall = self.span // self.depth
        self.half = slab // 2
        self.out_steps = steps_of(self.depth)
        self.back_steps = [list(reversed(pair)) for pair in reversed(self.out_steps)]
        self.pairs = len(self.out_steps)
        self.wide = block // SPLIT
        self.land_row = SLOT_ROW + self.groups
        self.matrix_row = self.land_row + matrices * self.columns
        self.table_rows = -(-(self.matrix_row + slots) // 8) * 8
        self.start = [self.lines * sum(map(len, self.back_steps[:a])) for a in range(self.pairs)]


def dot(a, b, dims=((1,), (0,))):
    return lax.dot_general(a, b, (dims, ((), ())), preferred_element_type=F32)


def fold(rows):
    line = jnp.sum(rows, axis=0, keepdims=True)
    total = line[:, :128]
    for at in range(128, line.shape[1], 128):
        total = total + line[:, at : at + 128]
    return total


def kernel(p, owners, grad, old, upd, new, *scratch):
    (mine, theirs, gsum, send_a, land_a, send_b, blocks, eye, root, other, half_out) = scratch[:11]
    (land_c, send_d, land_d, sums, scales, sums_z, sums_l, sums_c, draft, tab, stat, made, listed, whole, land_e) = scratch[11:26]
    (load_g, load_o, save_n, save_u, pair_s, pair_r, a_s, a_r, b_s, b_r) = scratch[26:36]
    (x_s, x_r, root_s, root_r, c_s, c_r, d_s, d_r, y_s, y_r) = scratch[36:46]
    (qz_s, qz_r, ql_s, ql_r, qc_s, qc_r, tab_s, list_s, p_s, p_r) = scratch[46:]

    depth, lines, slots, block = p.depth, p.lines, p.slots, p.block
    half, tall, columns, wide, pairs = p.half, p.tall, p.columns, p.wide, p.pairs
    me = lax.axis_index("fsdp")
    core = lax.axis_index("rep")
    far_core = 1 - core
    line = lax.div(me, depth)
    place = lax.rem(me, depth)
    ahead = [lax.rem(place + k, depth) for k in range(depth)]
    behind = [lax.rem(place + depth - k, depth) for k in range(depth)]
    partner = (me, far_core)

    def at(other_line, other_place):
        return (other_line * depth + other_place, core)

    def remote(src, dst, send, recv, device):
        return pltpu.make_async_remote_copy(
            src_ref=src, dst_ref=dst, send_sem=send, recv_sem=recv,
            device_id=device, device_id_type=MESH,
        )

    def landed(ref, sem):
        pltpu.make_async_copy(ref, ref, sem).wait()

    my_rows = pl.ds(pl.multiple_of(core * half, half), half)
    far_rows = pl.ds(pl.multiple_of(far_core * half, half), half)

    barrier = pltpu.get_barrier_semaphore()

    def greet(device):
        pl.semaphore_signal(barrier, inc=1, device_id=device, device_id_type=MESH)

    greet(partner)

    @pl.loop(1, depth)
    def _(step):
        greet(at(line, lax.rem(place + step, depth)))

    @pl.loop(1, lines)
    def _(step):
        greet(at(lax.rem(line + step, lines), place))

    listing = pltpu.make_async_copy(owners, listed, list_s)
    listing.start()
    part_of = p.matrices // SPLIT

    def cut(q, c=0):
        return pl.ds(c * block + q * wide, wide)

    for q in range(SPLIT):
        for c in range(columns):
            pltpu.make_async_copy(
                grad.at[0, :, my_rows, cut(q, c)], mine.at[:, :, cut(q, c)], load_g.at[q]
            ).start()
    for j in range(slots):
        pltpu.make_async_copy(old.at[0, j], stat.at[j], load_o.at[j]).start()
    sums[...] = jnp.zeros_like(sums)
    listing.wait()
    lookup = tables(p, listed[...], me, line, place)
    for row, value in lookup:
        draft[row : row + value.shape[0], :] = value
    pltpu.make_async_copy(draft, tab, tab_s).start()
    row_id = lax.broadcasted_iota(jnp.int32, (block, block), 0)
    col_id = lax.broadcasted_iota(jnp.int32, (block, block), 1)
    eye[...] = jnp.where(row_id == col_id, COEF[0], 0.0)
    pl.semaphore_wait(barrier, depth + lines - 1)

    for q in range(SPLIT):
        for c in range(columns):
            remote(
                grad.at[0, :, far_rows, cut(q, c)], theirs.at[:, :, cut(q, c)],
                pair_s.at[q], pair_r.at[q], partner,
            ).start()

    def add(q):
        landed(mine.at[pl.ds(0, part_of)], load_g.at[q])
        landed(theirs.at[pl.ds(0, part_of)], pair_r.at[q])

        @pl.loop(0, p.matrices)
        def _(m):
            square = jnp.zeros((half, wide), F32)
            for c in range(columns):
                value = mine[m, :, cut(q, c)].astype(F32) + theirs[m, :, cut(q, c)].astype(F32)
                value = value.astype(BF16)
                gsum[q][m * columns + c] = value
                value = value.astype(F32)
                square = square + value * value
            sums[0, pl.ds(m, 1), :] = sums[0, pl.ds(m, 1), :] + fold(square)

    add(0)
    landed(tab, tab_s)

    def across(q, a, pair):
        @pl.loop(0, lines, unroll=4)
        def _(to):
            for i, k in enumerate(pair):
                send_a[q][a][to, i] = gsum[q][tab[0, to * depth + ahead[k]]]

        @pl.loop(1, lines, unroll=5)
        def _(step):
            to = lax.rem(line + step, lines)
            remote(
                send_a[q][a].at[to], land_a[q][a].at[line],
                a_s.at[q * pairs + a], a_r.at[q * pairs + a], at(to, place),
            ).start()

        for i in range(len(pair)):
            land_a[q][a][line, i] = send_a[q][a][line, i]

    def along(q, a, pair):
        landed(land_a[q][a].at[pl.ds(0, lines - 1)], a_r.at[q * pairs + a])
        for i, k in enumerate(pair):
            to = ahead[k]
            for j in range(slots):
                group = tab[GROUP_ROW + j, line * depth + to]
                for t in range(tall):
                    piece = land_a[q][a][group * tall + t, i]
                    if k:
                        send_b[q, k - 1, j, t] = piece
                    else:
                        blocks[j, t, place, core, :, cut(q)] = piece
            if k:
                remote(
                    send_b.at[q, k - 1], blocks.at[:, :, place, core, :, cut(q)],
                    b_s.at[q * depth + k], b_r.at[q * depth + k], at(line, to),
                ).start()

    out_order = [(q, a, pair) for q in range(SPLIT) for a, pair in enumerate(p.out_steps)]
    for at_step in range(len(out_order) + AHEAD):
        if at_step % pairs == min(2, pairs - 1) and at_step // pairs + 1 < SPLIT:
            add(at_step // pairs + 1)
        if at_step < len(out_order):
            across(*out_order[at_step])
        if at_step >= AHEAD:
            along(*out_order[at_step - AHEAD])

    for q, _, pair in out_order:
        for k in pair:
            rows = blocks.at[:, :, behind[k], core, :, cut(q)]
            sem = q * depth + k
            if k:
                landed(rows, b_r.at[sem])
            remote(rows, rows, x_s.at[sem], x_r.at[sem], partner).start()
    for q, _, pair in out_order:
        for k in pair:
            landed(blocks.at[:, :, behind[k], far_core, :, cut(q)], x_r.at[q * depth + k])

    share = slots // 2
    assert share == 2

    @pl.loop(0, 2)
    def _(turn):
        first = lax.rem(turn + far_core, 2) * share
        both = [first, first + 1]
        for j in both:
            landed(stat.at[j], load_o.at[j])

        def statistics(dims):
            for j in both:
                g = blocks[j].reshape(block, block)
                stat[j] = DECAY_RATE * stat[j] + dot(g, g, dims)
                pltpu.make_async_copy(stat.at[j], new.at[0, j], save_n.at[j]).start()

        pl.when(core == 0)(lambda: statistics(((1,), (1,))))
        pl.when(core == 1)(lambda: statistics(((0,), (0,))))

        def each(f, *lists):
            return [f(*values) for values in zip(*lists)]

        a = [stat[j] for j in both]
        norm2 = each(
            lambda a: jnp.sum(jnp.sum(a * a, axis=0, keepdims=True), axis=1, keepdims=True) + EPSILON, a
        )
        norm = each(jnp.sqrt, norm2)
        inverse = each(lambda n: 1.0 / n, norm)
        b1 = each(lambda a, v: (a * v).astype(BF16), a, inverse)
        m2 = each(dot, b1, b1)
        b2 = each(lambda m: m.astype(BF16), m2)
        m3 = each(dot, b1, b2)
        b3 = each(lambda m: m.astype(BF16), m3)
        c4, c5, c6 = (jnp.asarray(v, BF16) for v in COEF[4:])
        upper = each(lambda x, y, w: c4 * x + c5 * y + c6 * w, b1, b2, b3)
        high = each(dot, b3, upper)
        low = each(
            lambda a, v, m2, m3: (COEF[1] * v) * a + COEF[2] * m2 + COEF[3] * m3 + eye[...],
            a, inverse, m2, m3,
        )
        x = each(lambda h, l, n: ((h + l) * lax.rsqrt(jnp.sqrt(n))).astype(BF16), high, low, norm)
        for j, value in zip(both, x):
            root[j] = value.reshape(root.shape[1:])

        @pl.when(turn == 0)
        def _():
            for i, j in enumerate(both):
                remote(root.at[j], other.at[i], root_s.at[i], root_r.at[i], partner).start()

    def apply(j, left, right):
        g = blocks[j].reshape(block, block)
        part = dot(g, right.reshape(block, block)).astype(BF16)
        return dot(left.reshape(block, block), part).astype(BF16).reshape(whole.shape[1:])

    matrix_id = lax.broadcasted_iota(jnp.int32, sums.shape[1:], 0)
    for i in range(share):
        j = core * share + i
        landed(other.at[i], root_r.at[i])

        @pl.when(core == 0)
        def _():
            whole[i] = apply(j, root[j], other[i])

        @pl.when(core == 1)
        def _():
            whole[i] = apply(j, other[i], root[j])

        remote(whole.at[i, :, :, far_core], half_out.at[j], p_s.at[i], p_r.at[i], partner).start()
        half_out[j] = whole[i, :, :, core]
        value = whole[i].reshape(block, block).astype(F32)
        total = fold(value * value)
        sums[1] = sums[1] + jnp.where(matrix_id == tab[p.matrix_row + j, me], total, 0.0)
    for i in range(share):
        landed(half_out.at[far_core * share + i], p_r.at[i])

    sums_z[place] = sums[...]

    @pl.loop(1, depth)
    def _(step):
        remote(sums, sums_z.at[place], qz_s, qz_r, at(line, lax.rem(place + step, depth))).start()

    back_order = [(q, a, pair) for q in range(SPLIT) for a, pair in enumerate(p.back_steps)]
    for q, _, pair in back_order:
        for k in pair:
            if k:
                to, sem = behind[k], q * depth + k
                remote(
                    half_out.at[:, :, to, :, cut(q)], land_c[q][k - 1], c_s.at[sem], c_r.at[sem], at(line, to)
                ).start()

    def back_across(q, a, pair):
        for k in pair:
            if k:
                landed(land_c[q][k - 1], c_r.at[q * depth + k])

        @pl.loop(0, lines, unroll=4)
        def _(to):
            for i, k in enumerate(pair):
                slot = tab[SLOT_ROW + lax.div(to, tall), line * depth + ahead[k]]
                if k:
                    send_d[q][a][to, i] = land_c[q][k - 1][slot, lax.rem(to, tall)]
                else:
                    send_d[q][a][to, i] = half_out[slot, lax.rem(to, tall), place, :, cut(q)]

        spot = pl.ds(p.start[a] + line * len(pair), len(pair))

        @pl.loop(1, lines, unroll=5)
        def _(step):
            to = lax.rem(line + step, lines)
            remote(
                send_d[q][a].at[to], land_d[q].at[spot],
                d_s.at[q * pairs + a], d_r.at[q * pairs + a], at(to, place),
            ).start()

        land_d[q][spot] = send_d[q][a][line]

    def back_pair(q, a, pair):
        sem = q * pairs + a
        landed(land_d[q].at[pl.ds(0, (lines - 1) * len(pair))], d_r.at[sem])
        rows = pl.ds(p.start[a], lines * len(pair))
        remote(land_d[q].at[rows], land_e[q].at[rows], y_s.at[sem], y_r.at[sem], partner).start()

    def far_landed(q):
        for a, pair in enumerate(p.back_steps):
            rows = pl.ds(p.start[a], lines * len(pair))
            landed(land_e[q].at[rows], y_r.at[q * pairs + a])

    def place_rows(q, h, source, m):
        factor = scales[pl.ds(m, 1), :]
        rows = pl.ds(pl.multiple_of(h * half, half), half)
        for c in range(columns):
            piece = source[q][tab[p.land_row + m * columns + c, 0]].astype(F32) * factor
            made[m, rows, cut(q, c)] = piece.astype(BF16)

    def place_both(q):
        far_landed(q)

        @pl.loop(0, p.matrices)
        def _(m):
            place_rows(q, core, land_d, m)
            place_rows(q, far_core, land_e, m)

    def find_scales():
        landed(sums_c.at[1], qc_r)
        total = jnp.sum(sums_c[0] + sums_c[1], axis=2, keepdims=True)
        count = float(p.slab * p.fsdp * p.model)
        scale = jnp.sqrt((total[0] / count + EPSILON) / (total[1] / count + EPSILON))
        scales[...] = jnp.broadcast_to(scale, scales.shape)

    for a in range(len(back_order) + AHEAD):
        if a < len(back_order):
            back_across(*back_order[a])
        if a == 1:
            landed(sums_z.at[pl.ds(0, depth - 1)], qz_r)
            sums_l[line] = jnp.sum(sums_z[...], axis=0)

            @pl.loop(1, lines)
            def _(step):
                remote(sums_l.at[line], sums_l.at[line], ql_s, ql_r, at(lax.rem(line + step, lines), place)).start()

        if a == pairs - 1:
            landed(sums_l.at[pl.ds(0, lines - 1)], ql_r)
            sums_c[0] = jnp.sum(sums_l[...], axis=0)
            remote(sums_c.at[0], sums_c.at[1], qc_s, qc_r, partner).start()
        if a == len(back_order):
            find_scales()
            for q in range(SPLIT - 1):
                place_both(q)
        if a >= AHEAD:
            back_pair(*back_order[a - AHEAD])

    last = SPLIT - 1

    @pl.loop(0, p.matrices)
    def _(m):
        place_rows(last, core, land_d, m)

    far_landed(last)

    @pl.loop(0, p.matrices)
    def _(m):
        place_rows(last, far_core, land_e, m)
        pltpu.make_async_copy(made.at[m], upd.at[m], save_u.at[m]).start()

    for q in range(SPLIT):
        landed(theirs.at[pl.ds(0, part_of)], pair_s.at[q])
        for a, pair in enumerate(p.out_steps):
            landed(send_a[q][a].at[pl.ds(0, lines - 1)], a_s.at[q * pairs + a])
        for a, pair in enumerate(p.back_steps):
            landed(send_d[q][a].at[pl.ds(0, lines - 1)], d_s.at[q * pairs + a])
            landed(land_d[q].at[pl.ds(p.start[a], lines * len(pair))], y_s.at[q * pairs + a])
        for k in range(depth):
            landed(blocks.at[:, :, behind[k], core, :, cut(q)], x_s.at[q * depth + k])
            if k:
                landed(send_b.at[q, k - 1], b_s.at[q * depth + k])
                landed(land_c[q][k - 1], c_s.at[q * depth + k])
    for j in range(slots):
        landed(stat.at[j], save_n.at[j])
    for i in range(share):
        landed(root.at[i], root_s.at[i])
        landed(whole.at[i, :, :, far_core], p_s.at[i])
    landed(sums_z.at[pl.ds(0, depth - 1)], qz_s)
    landed(sums_l.at[pl.ds(0, lines - 1)], ql_s)
    landed(sums_c.at[0], qc_s)
    for m in range(p.matrices):
        landed(made.at[m], save_u.at[m])


def tables(p, owner, me, line, place):
    groups, columns, lines, depth = p.groups, p.columns, p.lines, p.depth

    def bits(n):
        assert n & (n - 1) == 0
        return n.bit_length() - 1

    group = lax.shift_right_logical(owner, bits(columns)) & (groups - 1)
    matrix = lax.shift_right_logical(owner, bits(columns * groups))
    local = matrix * columns + (owner & (columns - 1))
    code = jnp.zeros((1, p.fsdp), jnp.int32)
    for j in range(p.slots):
        here = group[j : j + 1] == lax.div(me, p.span)
        code = code + jnp.where(here, local[j : j + 1] + 1, 0)
    group_id = lax.broadcasted_iota(jnp.int32, (groups, p.fsdp), 0)
    slot = jnp.zeros((groups, p.fsdp), jnp.int32)
    for j in range(1, p.slots):
        slot = slot + jnp.where(group[j : j + 1] == group_id, j, 0)
    lane = lax.broadcasted_iota(jnp.int32, (1, p.fsdp), 1)
    gap = ((lane & (depth - 1)) - place) & (depth - 1)
    land = jnp.zeros((1, p.fsdp), jnp.int32)
    for a, pair in enumerate(p.back_steps):
        for i, k in enumerate(pair):
            spot = p.start[a] + lax.shift_right_logical(lane, bits(depth)) * len(pair) + i
            land = land + jnp.where(gap == k, spot, 0)
    block_id = lax.broadcasted_iota(jnp.int32, (p.matrices * columns, p.fsdp), 0)
    hit = jnp.where(code == block_id + 1, land, 0)
    hit = jnp.broadcast_to(jnp.sum(hit, axis=1, keepdims=True), hit.shape)
    return [
        (0, jnp.clip(code - 1, 0, p.matrices * columns - 1)),
        (GROUP_ROW, group),
        (SLOT_ROW, jnp.minimum(slot, p.slots - 1)),
        (p.land_row, jnp.minimum(hit, lines * depth - 1)),
        (p.matrix_row, matrix),
    ]


def body(p, gradient, old_stats, owner_table):
    depth, lines, slots, block = p.depth, p.lines, p.slots, p.block
    half, tall, wide = p.half, p.tall, p.wide
    pairs, steps = SPLIT * p.pairs, SPLIT * depth
    dma = pltpu.SemaphoreType.DMA
    vm = pltpu.VMEM
    full = (slots, tall, depth, 2, half, block)

    def chunks(order):
        return [[vm((lines, len(pair), half, wide), BF16) for pair in order] for _ in range(SPLIT)]

    scratch = [
        vm((p.matrices, half, p.model), BF16),
        vm((p.matrices, half, p.model), BF16),
        [vm((p.matrices * p.columns, half, wide), BF16) for _ in range(SPLIT)],
        chunks(p.out_steps),
        chunks(p.out_steps),
        vm((SPLIT, depth - 1, slots, tall, half, wide), BF16),
        vm(full, BF16),
        vm((block, block), F32),
        vm(full, BF16),
        vm((2,) + full[1:], BF16),
        vm((slots, tall, depth, half, block), BF16),
        [[vm((slots, tall, half, wide), BF16) for _ in range(depth - 1)] for _ in range(SPLIT)],
        chunks(p.back_steps),
        [vm((lines * depth, half, wide), BF16) for _ in range(SPLIT)],
        vm((2, p.matrices, 128), F32),
        vm((p.matrices, wide), F32),
        vm((depth, 2, p.matrices, 128), F32),
        vm((lines, 2, p.matrices, 128), F32),
        vm((2, 2, p.matrices, 128), F32),
        vm((p.table_rows, p.fsdp), jnp.int32),
        pltpu.SMEM((p.table_rows, p.fsdp), jnp.int32),
        vm((slots, block, block), F32),
        vm((p.matrices, p.slab, p.model), BF16),
        vm((slots, p.fsdp), jnp.int32),
        vm((2,) + full[1:], BF16),
        [vm((lines * depth, half, wide), BF16) for _ in range(SPLIT)],
    ]
    counts = [SPLIT, slots, slots, p.matrices, SPLIT, SPLIT, pairs, pairs, steps, steps]
    counts += [steps, steps, 2, 2, steps, steps, pairs, pairs, pairs, pairs]
    scratch += [dma((count,)) for count in counts]
    scratch += [dma] * 8 + [dma((2,))] * 2
    update, fresh = pl.pallas_call(
        functools.partial(kernel, p),
        out_shape=(
            jax.ShapeDtypeStruct((p.matrices, p.slab, p.model), BF16),
            jax.ShapeDtypeStruct(old_stats.shape, F32),
        ),
        in_specs=[
            pl.BlockSpec(memory_space=pltpu.HBM),
            pl.BlockSpec(memory_space=pltpu.HBM),
            pl.BlockSpec(memory_space=pltpu.HBM),
        ],
        out_specs=(pl.BlockSpec(memory_space=pl.ANY), pl.BlockSpec(memory_space=pl.ANY)),
        scratch_shapes=scratch,
        compiler_params=pltpu.CompilerParams(
            collective_id=0, has_side_effects=True, vmem_limit_bytes=VMEM_BYTES
        ),
        name="shampoo",
    )(*(pltpu.with_memory_space_constraint(x, pltpu.HBM) for x in (owner_table.T, gradient, old_stats)))
    return update, fresh


def solution(mesh):
    def whole(gradient, old_stats, owner_table):
        fsdp = mesh.shape["fsdp"]
        _, matrices, rows, model = gradient.shape
        p = Plan(fsdp, matrices, rows // fsdp, model, owner_table.shape[1], old_stats.shape[2])
        return jax.shard_map(
            functools.partial(body, p),
            mesh=mesh,
            in_specs=(P("rep", None, "fsdp", None), P("rep", "fsdp", None, None), P()),
            out_specs=(P(None, "fsdp", None), P("rep", "fsdp", None, None)),
            check_vma=False,
        )(gradient, old_stats, owner_table)

    return whole
```

```python
import functools

import jax
import jax.numpy as jnp
from jax import lax
from jax.experimental import pallas as pl
from jax.experimental.pallas import tpu as pltpu
from jax.sharding import PartitionSpec as P

DECAY_RATE = 0.95
EPSILON = 1e-06
MESH = pl.DeviceIdType.MESH
F32 = jnp.float32
BF16 = jnp.bfloat16
VMEM_BYTES = 44 * 1024 * 1024

DEPTH = 8
GROUP_ROW, SLOT_ROW = 8, 16
AHEAD = 5
SPLIT = 2

COEF = tuple(
    v / 4096.0 for v in (6400.0, -4405.0, 3125.0, -1250.0, 250.0, -25.0, 1.0)
)


def steps_of(depth):
    pairs = [[low, depth - low] for low in range(depth // 2 - 1, 0, -1)]
    return [[depth // 2]] + pairs + [[0]]


class Plan:
    def __init__(self, fsdp, matrices, slab, model, slots, block):
        self.fsdp, self.matrices, self.slab, self.model = fsdp, matrices, slab, model
        self.slots, self.block = slots, block
        self.depth = DEPTH
        self.lines = fsdp // self.depth
        self.columns = model // block
        self.span = block // slab
        self.groups = fsdp // self.span
        self.tall = self.span // self.depth
        self.half = slab // 2
        self.out_steps = steps_of(self.depth)
        self.back_steps = [list(reversed(pair)) for pair in reversed(self.out_steps)]
        self.pairs = len(self.out_steps)
        self.wide = block // SPLIT
        self.land_row = SLOT_ROW + self.groups
        self.matrix_row = self.land_row + matrices * self.columns
        self.table_rows = -(-(self.matrix_row + slots) // 8) * 8
        self.start = [self.lines * sum(map(len, self.back_steps[:a])) for a in range(self.pairs)]


def dot(a, b, dims=((1,), (0,))):
    return lax.dot_general(a, b, (dims, ((), ())), preferred_element_type=F32)


def fold(rows):
    line = jnp.sum(rows, axis=0, keepdims=True)
    total = line[:, :128]
    for at in range(128, line.shape[1], 128):
        total = total + line[:, at : at + 128]
    return total


def kernel(p, owners, grad, old, upd, new, *scratch):
    (mine, theirs, gsum, send_a, land_a, send_b, blocks, eye, root, other, half_out) = scratch[:11]
    (land_c, send_d, land_d, sums, scales, sums_z, sums_l, sums_c, draft, tab, stat, made, listed, whole, land_e) = scratch[11:26]
    (load_g, load_o, save_n, save_u, pair_s, pair_r, a_s, a_r, b_s, b_r) = scratch[26:36]
    (x_s, x_r, root_s, root_r, c_s, c_r, d_s, d_r, y_s, y_r) = scratch[36:46]
    (qz_s, qz_r, ql_s, ql_r, qc_s, qc_r, tab_s, list_s, p_s, p_r) = scratch[46:]

    depth, lines, slots, block = p.depth, p.lines, p.slots, p.block
    half, tall, columns, wide, pairs = p.half, p.tall, p.columns, p.wide, p.pairs
    me = lax.axis_index("fsdp")
    core = lax.axis_index("rep")
    far_core = 1 - core
    line = lax.div(me, depth)
    place = lax.rem(me, depth)
    ahead = [lax.rem(place + k, depth) for k in range(depth)]
    behind = [lax.rem(place + depth - k, depth) for k in range(depth)]
    partner = (me, far_core)

    def at(other_line, other_place):
        return (other_line * depth + other_place, core)

    def remote(src, dst, send, recv, device):
        return pltpu.make_async_remote_copy(
            src_ref=src, dst_ref=dst, send_sem=send, recv_sem=recv,
            device_id=device, device_id_type=MESH,
        )

    def landed(ref, sem):
        pltpu.make_async_copy(ref, ref, sem).wait()

    my_rows = pl.ds(pl.multiple_of(core * half, half), half)
    far_rows = pl.ds(pl.multiple_of(far_core * half, half), half)

    barrier = pltpu.get_barrier_semaphore()

    def greet(device):
        pl.semaphore_signal(barrier, inc=1, device_id=device, device_id_type=MESH)

    greet(partner)

    @pl.loop(1, depth)
    def _(step):
        greet(at(line, lax.rem(place + step, depth)))

    @pl.loop(1, lines)
    def _(step):
        greet(at(lax.rem(line + step, lines), place))

    listing = pltpu.make_async_copy(owners, listed, list_s)
    listing.start()
    part_of = p.matrices // SPLIT

    def cut(q, c=0):
        return pl.ds(c * block + q * wide, wide)

    for q in range(SPLIT):
        for c in range(columns):
            pltpu.make_async_copy(
                grad.at[0, :, my_rows, cut(q, c)], mine.at[:, :, cut(q, c)], load_g.at[q]
            ).start()
    for j in range(slots):
        pltpu.make_async_copy(old.at[0, j], stat.at[j], load_o.at[j]).start()
    sums[...] = jnp.zeros_like(sums)
    listing.wait()
    lookup = tables(p, listed[...], me, line, place)
    for row, value in lookup:
        draft[row : row + value.shape[0], :] = value
    pltpu.make_async_copy(draft, tab, tab_s).start()
    row_id = lax.broadcasted_iota(jnp.int32, (block, block), 0)
    col_id = lax.broadcasted_iota(jnp.int32, (block, block), 1)
    eye[...] = jnp.where(row_id == col_id, COEF[0], 0.0)
    pl.semaphore_wait(barrier, depth + lines - 1)

    for q in range(SPLIT):
        for c in range(columns):
            remote(
                grad.at[0, :, far_rows, cut(q, c)], theirs.at[:, :, cut(q, c)],
                pair_s.at[q], pair_r.at[q], partner,
            ).start()

    def add(q):
        landed(mine.at[pl.ds(0, part_of)], load_g.at[q])
        landed(theirs.at[pl.ds(0, part_of)], pair_r.at[q])

        @pl.loop(0, p.matrices)
        def _(m):
            square = jnp.zeros((half, wide), F32)
            for c in range(columns):
                value = mine[m, :, cut(q, c)].astype(F32) + theirs[m, :, cut(q, c)].astype(F32)
                value = value.astype(BF16)
                gsum[q][m * columns + c] = value
                value = value.astype(F32)
                square = square + value * value
            sums[0, pl.ds(m, 1), :] = sums[0, pl.ds(m, 1), :] + fold(square)

    add(0)
    landed(tab, tab_s)

    def across(q, a, pair):
        @pl.loop(0, lines, unroll=4)
        def _(to):
            for i, k in enumerate(pair):
                send_a[q][a][to, i] = gsum[q][tab[0, to * depth + ahead[k]]]

        @pl.loop(1, lines, unroll=5)
        def _(step):
            to = lax.rem(line + step, lines)
            remote(
                send_a[q][a].at[to], land_a[q][a].at[line],
                a_s.at[q * pairs + a], a_r.at[q * pairs + a], at(to, place),
            ).start()

        for i in range(len(pair)):
            land_a[q][a][line, i] = send_a[q][a][line, i]

    def along(q, a, pair):
        landed(land_a[q][a].at[pl.ds(0, lines - 1)], a_r.at[q * pairs + a])
        for i, k in enumerate(pair):
            to = ahead[k]
            for j in range(slots):
                group = tab[GROUP_ROW + j, line * depth + to]
                for t in range(tall):
                    piece = land_a[q][a][group * tall + t, i]
                    if k:
                        send_b[q, k - 1, j, t] = piece
                    else:
                        blocks[j, t, place, core, :, cut(q)] = piece
            if k:
                remote(
                    send_b.at[q, k - 1], blocks.at[:, :, place, core, :, cut(q)],
                    b_s.at[q * depth + k], b_r.at[q * depth + k], at(line, to),
                ).start()

    out_order = [(q, a, pair) for q in range(SPLIT) for a, pair in enumerate(p.out_steps)]

    def pair_up(q, _, pair):
        for k in pair:
            rows = blocks.at[:, :, behind[k], core, :, cut(q)]
            sem = q * depth + k
            if k:
                landed(rows, b_r.at[sem])
            remote(rows, rows, x_s.at[sem], x_r.at[sem], partner).start()

    late = AHEAD + 3
    for at_step in range(len(out_order) + late):
        if at_step % pairs == min(2, pairs - 1) and at_step // pairs + 1 < SPLIT:
            add(at_step // pairs + 1)
        if at_step < len(out_order):
            across(*out_order[at_step])
        if AHEAD <= at_step < len(out_order) + AHEAD:
            along(*out_order[at_step - AHEAD])
        if at_step >= late:
            pair_up(*out_order[at_step - late])

    for q, _, pair in out_order:
        for k in pair:
            landed(blocks.at[:, :, behind[k], far_core, :, cut(q)], x_r.at[q * depth + k])

    share = slots // 2
    assert share == 2

    @pl.loop(0, 2)
    def _(turn):
        first = lax.rem(turn + far_core, 2) * share
        both = [first, first + 1]
        for j in both:
            landed(stat.at[j], load_o.at[j])

        def statistics(dims):
            for j in both:
                g = blocks[j].reshape(block, block)
                stat[j] = DECAY_RATE * stat[j] + dot(g, g, dims)
                pltpu.make_async_copy(stat.at[j], new.at[0, j], save_n.at[j]).start()

        pl.when(core == 0)(lambda: statistics(((1,), (1,))))
        pl.when(core == 1)(lambda: statistics(((0,), (0,))))

        def each(f, *lists):
            return [f(*values) for values in zip(*lists)]

        a = [stat[j] for j in both]
        norm2 = each(
            lambda a: jnp.sum(jnp.sum(a * a, axis=0, keepdims=True), axis=1, keepdims=True) + EPSILON, a
        )
        norm = each(jnp.sqrt, norm2)
        inverse = each(lambda n: 1.0 / n, norm)
        b1 = each(lambda a, v: (a * v).astype(BF16), a, inverse)
        m2 = each(dot, b1, b1)
        b2 = each(lambda m: m.astype(BF16), m2)
        m3 = each(dot, b1, b2)
        b3 = each(lambda m: m.astype(BF16), m3)
        c4, c5, c6 = (jnp.asarray(v, BF16) for v in COEF[4:])
        upper = each(lambda x, y, w: c4 * x + c5 * y + c6 * w, b1, b2, b3)
        high = each(dot, b3, upper)
        low = each(
            lambda a, v, m2, m3: (COEF[1] * v) * a + COEF[2] * m2 + COEF[3] * m3 + eye[...],
            a, inverse, m2, m3,
        )
        x = each(lambda h, l, n: ((h + l) * lax.rsqrt(jnp.sqrt(n))).astype(BF16), high, low, norm)
        for j, value in zip(both, x):
            root[j] = value.reshape(root.shape[1:])

        @pl.when(turn == 0)
        def _():
            for i, j in enumerate(both):
                remote(root.at[j], other.at[i], root_s.at[i], root_r.at[i], partner).start()

    def apply(j, left, right):
        g = blocks[j].reshape(block, block)
        part = dot(g, right.reshape(block, block)).astype(BF16)
        return dot(left.reshape(block, block), part).astype(BF16).reshape(whole.shape[1:])

    matrix_id = lax.broadcasted_iota(jnp.int32, sums.shape[1:], 0)
    for i in range(share):
        j = core * share + i
        landed(other.at[i], root_r.at[i])

        @pl.when(core == 0)
        def _():
            whole[i] = apply(j, root[j], other[i])

        @pl.when(core == 1)
        def _():
            whole[i] = apply(j, other[i], root[j])

        remote(whole.at[i, :, :, far_core], half_out.at[j], p_s.at[i], p_r.at[i], partner).start()
        half_out[j] = whole[i, :, :, core]
        value = whole[i].reshape(block, block).astype(F32)
        total = fold(value * value)
        sums[1] = sums[1] + jnp.where(matrix_id == tab[p.matrix_row + j, me], total, 0.0)
    for i in range(share):
        landed(half_out.at[far_core * share + i], p_r.at[i])

    sums_z[place] = sums[...]

    @pl.loop(1, depth)
    def _(step):
        remote(sums, sums_z.at[place], qz_s, qz_r, at(line, lax.rem(place + step, depth))).start()

    back_order = [(q, a, pair) for q in range(SPLIT) for a, pair in enumerate(p.back_steps)]
    for q, _, pair in back_order:
        for k in pair:
            if k:
                to, sem = behind[k], q * depth + k
                remote(
                    half_out.at[:, :, to, :, cut(q)], land_c[q][k - 1], c_s.at[sem], c_r.at[sem], at(line, to)
                ).start()

    def back_across(q, a, pair):
        for k in pair:
            if k:
                landed(land_c[q][k - 1], c_r.at[q * depth + k])

        @pl.loop(0, lines, unroll=4)
        def _(to):
            for i, k in enumerate(pair):
                slot = tab[SLOT_ROW + lax.div(to, tall), line * depth + ahead[k]]
                if k:
                    send_d[q][a][to, i] = land_c[q][k - 1][slot, lax.rem(to, tall)]
                else:
                    send_d[q][a][to, i] = half_out[slot, lax.rem(to, tall), place, :, cut(q)]

        spot = pl.ds(p.start[a] + line * len(pair), len(pair))

        @pl.loop(1, lines, unroll=5)
        def _(step):
            to = lax.rem(line + step, lines)
            remote(
                send_d[q][a].at[to], land_d[q].at[spot],
                d_s.at[q * pairs + a], d_r.at[q * pairs + a], at(to, place),
            ).start()

        land_d[q][spot] = send_d[q][a][line]

    def back_pair(q, a, pair):
        sem = q * pairs + a
        landed(land_d[q].at[pl.ds(0, (lines - 1) * len(pair))], d_r.at[sem])
        rows = pl.ds(p.start[a], lines * len(pair))
        remote(land_d[q].at[rows], land_e[q].at[rows], y_s.at[sem], y_r.at[sem], partner).start()

    def far_landed(q):
        for a, pair in enumerate(p.back_steps):
            rows = pl.ds(p.start[a], lines * len(pair))
            landed(land_e[q].at[rows], y_r.at[q * pairs + a])

    def place_rows(q, h, source, m):
        factor = scales[pl.ds(m, 1), :]
        rows = pl.ds(pl.multiple_of(h * half, half), half)
        for c in range(columns):
            piece = source[q][tab[p.land_row + m * columns + c, 0]].astype(F32) * factor
            made[m, rows, cut(q, c)] = piece.astype(BF16)

    def place_both(q):
        far_landed(q)

        @pl.loop(0, p.matrices)
        def _(m):
            place_rows(q, core, land_d, m)
            place_rows(q, far_core, land_e, m)

    def find_scales():
        landed(sums_c.at[1], qc_r)
        total = jnp.sum(sums_c[0] + sums_c[1], axis=2, keepdims=True)
        count = float(p.slab * p.fsdp * p.model)
        scale = jnp.sqrt((total[0] / count + EPSILON) / (total[1] / count + EPSILON))
        scales[...] = jnp.broadcast_to(scale, scales.shape)

    for a in range(len(back_order) + AHEAD):
        if a < len(back_order):
            back_across(*back_order[a])
        if a == 1:
            landed(sums_z.at[pl.ds(0, depth - 1)], qz_r)
            sums_l[line] = jnp.sum(sums_z[...], axis=0)

            @pl.loop(1, lines)
            def _(step):
                remote(sums_l.at[line], sums_l.at[line], ql_s, ql_r, at(lax.rem(line + step, lines), place)).start()

        if a == pairs - 1:
            landed(sums_l.at[pl.ds(0, lines - 1)], ql_r)
            sums_c[0] = jnp.sum(sums_l[...], axis=0)
            remote(sums_c.at[0], sums_c.at[1], qc_s, qc_r, partner).start()
        if a == len(back_order):
            find_scales()
            for q in range(SPLIT - 1):
                place_both(q)
        if a >= AHEAD:
            back_pair(*back_order[a - AHEAD])

    last = SPLIT - 1

    @pl.loop(0, p.matrices)
    def _(m):
        place_rows(last, core, land_d, m)

    far_landed(last)

    @pl.loop(0, p.matrices)
    def _(m):
        place_rows(last, far_core, land_e, m)
        pltpu.make_async_copy(made.at[m], upd.at[m], save_u.at[m]).start()

    for q in range(SPLIT):
        landed(theirs.at[pl.ds(0, part_of)], pair_s.at[q])
        for a, pair in enumerate(p.out_steps):
            landed(send_a[q][a].at[pl.ds(0, lines - 1)], a_s.at[q * pairs + a])
        for a, pair in enumerate(p.back_steps):
            landed(send_d[q][a].at[pl.ds(0, lines - 1)], d_s.at[q * pairs + a])
            landed(land_d[q].at[pl.ds(p.start[a], lines * len(pair))], y_s.at[q * pairs + a])
        for k in range(depth):
            landed(blocks.at[:, :, behind[k], core, :, cut(q)], x_s.at[q * depth + k])
            if k:
                landed(send_b.at[q, k - 1], b_s.at[q * depth + k])
                landed(land_c[q][k - 1], c_s.at[q * depth + k])
    for j in range(slots):
        landed(stat.at[j], save_n.at[j])
    for i in range(share):
        landed(root.at[i], root_s.at[i])
        landed(whole.at[i, :, :, far_core], p_s.at[i])
    landed(sums_z.at[pl.ds(0, depth - 1)], qz_s)
    landed(sums_l.at[pl.ds(0, lines - 1)], ql_s)
    landed(sums_c.at[0], qc_s)
    for m in range(p.matrices):
        landed(made.at[m], save_u.at[m])


def tables(p, owner, me, line, place):
    groups, columns, lines, depth = p.groups, p.columns, p.lines, p.depth

    def bits(n):
        assert n & (n - 1) == 0
        return n.bit_length() - 1

    group = lax.shift_right_logical(owner, bits(columns)) & (groups - 1)
    matrix = lax.shift_right_logical(owner, bits(columns * groups))
    local = matrix * columns + (owner & (columns - 1))
    code = jnp.zeros((1, p.fsdp), jnp.int32)
    for j in range(p.slots):
        here = group[j : j + 1] == lax.div(me, p.span)
        code = code + jnp.where(here, local[j : j + 1] + 1, 0)
    group_id = lax.broadcasted_iota(jnp.int32, (groups, p.fsdp), 0)
    slot = jnp.zeros((groups, p.fsdp), jnp.int32)
    for j in range(1, p.slots):
        slot = slot + jnp.where(group[j : j + 1] == group_id, j, 0)
    lane = lax.broadcasted_iota(jnp.int32, (1, p.fsdp), 1)
    gap = ((lane & (depth - 1)) - place) & (depth - 1)
    land = jnp.zeros((1, p.fsdp), jnp.int32)
    for a, pair in enumerate(p.back_steps):
        for i, k in enumerate(pair):
            spot = p.start[a] + lax.shift_right_logical(lane, bits(depth)) * len(pair) + i
            land = land + jnp.where(gap == k, spot, 0)
    block_id = lax.broadcasted_iota(jnp.int32, (p.matrices * columns, p.fsdp), 0)
    hit = jnp.where(code == block_id + 1, land, 0)
    hit = jnp.broadcast_to(jnp.sum(hit, axis=1, keepdims=True), hit.shape)
    return [
        (0, jnp.clip(code - 1, 0, p.matrices * columns - 1)),
        (GROUP_ROW, group),
        (SLOT_ROW, jnp.minimum(slot, p.slots - 1)),
        (p.land_row, jnp.minimum(hit, lines * depth - 1)),
        (p.matrix_row, matrix),
    ]


def body(p, gradient, old_stats, owner_table):
    depth, lines, slots, block = p.depth, p.lines, p.slots, p.block
    half, tall, wide = p.half, p.tall, p.wide
    pairs, steps = SPLIT * p.pairs, SPLIT * depth
    dma = pltpu.SemaphoreType.DMA
    vm = pltpu.VMEM
    full = (slots, tall, depth, 2, half, block)

    def chunks(order):
        return [[vm((lines, len(pair), half, wide), BF16) for pair in order] for _ in range(SPLIT)]

    scratch = [
        vm((p.matrices, half, p.model), BF16),
        vm((p.matrices, half, p.model), BF16),
        [vm((p.matrices * p.columns, half, wide), BF16) for _ in range(SPLIT)],
        chunks(p.out_steps),
        chunks(p.out_steps),
        vm((SPLIT, depth - 1, slots, tall, half, wide), BF16),
        vm(full, BF16),
        vm((block, block), F32),
        vm(full, BF16),
        vm((2,) + full[1:], BF16),
        vm((slots, tall, depth, half, block), BF16),
        [[vm((slots, tall, half, wide), BF16) for _ in range(depth - 1)] for _ in range(SPLIT)],
        chunks(p.back_steps),
        [vm((lines * depth, half, wide), BF16) for _ in range(SPLIT)],
        vm((2, p.matrices, 128), F32),
        vm((p.matrices, wide), F32),
        vm((depth, 2, p.matrices, 128), F32),
        vm((lines, 2, p.matrices, 128), F32),
        vm((2, 2, p.matrices, 128), F32),
        vm((p.table_rows, p.fsdp), jnp.int32),
        pltpu.SMEM((p.table_rows, p.fsdp), jnp.int32),
        vm((slots, block, block), F32),
        vm((p.matrices, p.slab, p.model), BF16),
        vm((slots, p.fsdp), jnp.int32),
        vm((2,) + full[1:], BF16),
        [vm((lines * depth, half, wide), BF16) for _ in range(SPLIT)],
    ]
    counts = [SPLIT, slots, slots, p.matrices, SPLIT, SPLIT, pairs, pairs, steps, steps]
    counts += [steps, steps, 2, 2, steps, steps, pairs, pairs, pairs, pairs]
    scratch += [dma((count,)) for count in counts]
    scratch += [dma] * 8 + [dma((2,))] * 2
    update, fresh = pl.pallas_call(
        functools.partial(kernel, p),
        out_shape=(
            jax.ShapeDtypeStruct((p.matrices, p.slab, p.model), BF16),
            jax.ShapeDtypeStruct(old_stats.shape, F32),
        ),
        in_specs=[
            pl.BlockSpec(memory_space=pltpu.HBM),
            pl.BlockSpec(memory_space=pltpu.HBM),
            pl.BlockSpec(memory_space=pltpu.HBM),
        ],
        out_specs=(pl.BlockSpec(memory_space=pl.ANY), pl.BlockSpec(memory_space=pl.ANY)),
        scratch_shapes=scratch,
        compiler_params=pltpu.CompilerParams(
            collective_id=0, has_side_effects=True, vmem_limit_bytes=VMEM_BYTES
        ),
        name="shampoo",
    )(*(pltpu.with_memory_space_constraint(x, pltpu.HBM) for x in (owner_table.T, gradient, old_stats)))
    return update, fresh


def solution(mesh):
    def whole(gradient, old_stats, owner_table):
        fsdp = mesh.shape["fsdp"]
        _, matrices, rows, model = gradient.shape
        p = Plan(fsdp, matrices, rows // fsdp, model, owner_table.shape[1], old_stats.shape[2])
        return jax.shard_map(
            functools.partial(body, p),
            mesh=mesh,
            in_specs=(P("rep", None, "fsdp", None), P("rep", "fsdp", None, None), P()),
            out_specs=(P(None, "fsdp", None), P("rep", "fsdp", None, None)),
            check_vma=False,
        )(gradient, old_stats, owner_table)

    return whole
```

```python
import functools

import jax
import jax.numpy as jnp
from jax import lax
from jax.experimental import pallas as pl
from jax.experimental.pallas import tpu as pltpu
from jax.sharding import PartitionSpec as P

DECAY_RATE = 0.95
EPSILON = 1e-06
MESH = pl.DeviceIdType.MESH
F32 = jnp.float32
BF16 = jnp.bfloat16
VMEM_BYTES = 44 * 1024 * 1024

DEPTH = 8
GROUP_ROW, SLOT_ROW = 8, 16
AHEAD = 3
SPLIT = 2

COEF = tuple(
    v / 4096.0 for v in (6400.0, -4405.0, 3125.0, -1250.0, 250.0, -25.0, 1.0)
)


def steps_of(depth):
    pairs = [[low, depth - low] for low in range(depth // 2 - 1, 0, -1)]
    return [[depth // 2]] + pairs + [[0]]


class Plan:
    def __init__(self, fsdp, matrices, slab, model, slots, block):
        self.fsdp, self.matrices, self.slab, self.model = fsdp, matrices, slab, model
        self.slots, self.block = slots, block
        self.depth = DEPTH
        self.lines = fsdp // self.depth
        self.columns = model // block
        self.span = block // slab
        self.groups = fsdp // self.span
        self.tall = self.span // self.depth
        self.half = slab // 2
        self.out_steps = steps_of(self.depth)
        self.back_steps = [list(reversed(pair)) for pair in reversed(self.out_steps)]
        self.pairs = len(self.out_steps)
        self.wide = block // SPLIT
        self.land_row = SLOT_ROW + self.groups
        self.matrix_row = self.land_row + matrices * self.columns
        self.table_rows = -(-(self.matrix_row + slots) // 8) * 8
        self.start = [self.lines * sum(map(len, self.back_steps[:a])) for a in range(self.pairs)]


def dot(a, b, dims=((1,), (0,))):
    return lax.dot_general(a, b, (dims, ((), ())), preferred_element_type=F32)


def fold(rows):
    line = jnp.sum(rows, axis=0, keepdims=True)
    total = line[:, :128]
    for at in range(128, line.shape[1], 128):
        total = total + line[:, at : at + 128]
    return total


def kernel(p, owners, grad, old, upd, new, *scratch):
    (mine, theirs, gsum, send_a, land_a, send_b, blocks, eye, root, other, half_out) = scratch[:11]
    (land_c, send_d, land_d, sums, scales, sums_z, sums_l, sums_c, draft, tab, stat, made, listed, whole, land_e) = scratch[11:26]
    (load_g, load_o, save_n, save_u, pair_s, pair_r, a_s, a_r, b_s, b_r) = scratch[26:36]
    (x_s, x_r, root_s, root_r, c_s, c_r, d_s, d_r, y_s, y_r) = scratch[36:46]
    (qz_s, qz_r, ql_s, ql_r, qc_s, qc_r, tab_s, list_s, p_s, p_r) = scratch[46:]

    depth, lines, slots, block = p.depth, p.lines, p.slots, p.block
    half, tall, columns, wide, pairs = p.half, p.tall, p.columns, p.wide, p.pairs
    me = lax.axis_index("fsdp")
    core = lax.axis_index("rep")
    far_core = 1 - core
    line = lax.div(me, depth)
    place = lax.rem(me, depth)
    ahead = [lax.rem(place + k, depth) for k in range(depth)]
    behind = [lax.rem(place + depth - k, depth) for k in range(depth)]
    partner = (me, far_core)

    def at(other_line, other_place):
        return (other_line * depth + other_place, core)

    def remote(src, dst, send, recv, device):
        return pltpu.make_async_remote_copy(
            src_ref=src, dst_ref=dst, send_sem=send, recv_sem=recv,
            device_id=device, device_id_type=MESH,
        )

    def landed(ref, sem):
        pltpu.make_async_copy(ref, ref, sem).wait()

    my_rows = pl.ds(pl.multiple_of(core * half, half), half)
    far_rows = pl.ds(pl.multiple_of(far_core * half, half), half)

    barrier = pltpu.get_barrier_semaphore()

    def greet(device):
        pl.semaphore_signal(barrier, inc=1, device_id=device, device_id_type=MESH)

    greet(partner)

    @pl.loop(1, depth)
    def _(step):
        greet(at(line, lax.rem(place + step, depth)))

    @pl.loop(1, lines)
    def _(step):
        greet(at(lax.rem(line + step, lines), place))

    listing = pltpu.make_async_copy(owners, listed, list_s)
    listing.start()
    part_of = p.matrices // SPLIT

    def cut(q, c=0):
        return pl.ds(c * block + q * wide, wide)

    for q in range(SPLIT):
        for c in range(columns):
            pltpu.make_async_copy(
                grad.at[0, :, my_rows, cut(q, c)], mine.at[:, :, cut(q, c)], load_g.at[q]
            ).start()
    for j in range(slots):
        pltpu.make_async_copy(old.at[0, j], stat.at[j], load_o.at[j]).start()
    sums[...] = jnp.zeros_like(sums)
    listing.wait()
    lookup = tables(p, listed[...], me, line, place)
    for row, value in lookup:
        draft[row : row + value.shape[0], :] = value
    pltpu.make_async_copy(draft, tab, tab_s).start()
    row_id = lax.broadcasted_iota(jnp.int32, (block, block), 0)
    col_id = lax.broadcasted_iota(jnp.int32, (block, block), 1)
    eye[...] = jnp.where(row_id == col_id, COEF[0], 0.0)
    pl.semaphore_wait(barrier, depth + lines - 1)

    for q in range(SPLIT):
        for c in range(columns):
            remote(
                grad.at[0, :, far_rows, cut(q, c)], theirs.at[:, :, cut(q, c)],
                pair_s.at[q], pair_r.at[q], partner,
            ).start()

    def add(q):
        landed(mine.at[pl.ds(0, part_of)], load_g.at[q])
        landed(theirs.at[pl.ds(0, part_of)], pair_r.at[q])

        @pl.loop(0, p.matrices)
        def _(m):
            square = jnp.zeros((half, wide), F32)
            for c in range(columns):
                value = mine[m, :, cut(q, c)].astype(F32) + theirs[m, :, cut(q, c)].astype(F32)
                value = value.astype(BF16)
                gsum[q][m * columns + c] = value
                value = value.astype(F32)
                square = square + value * value
            sums[0, pl.ds(m, 1), :] = sums[0, pl.ds(m, 1), :] + fold(square)

    add(0)
    landed(tab, tab_s)

    def across(q, a, pair):
        @pl.loop(0, lines, unroll=4)
        def _(to):
            for i, k in enumerate(pair):
                send_a[q][a][to, i] = gsum[q][tab[0, to * depth + ahead[k]]]

        @pl.loop(1, lines, unroll=5)
        def _(step):
            to = lax.rem(line + step, lines)
            remote(
                send_a[q][a].at[to], land_a[q][a].at[line],
                a_s.at[q * pairs + a], a_r.at[q * pairs + a], at(to, place),
            ).start()

        for i in range(len(pair)):
            land_a[q][a][line, i] = send_a[q][a][line, i]

    def along(q, a, pair):
        landed(land_a[q][a].at[pl.ds(0, lines - 1)], a_r.at[q * pairs + a])
        for i, k in enumerate(pair):
            to = ahead[k]
            for j in range(slots):
                group = tab[GROUP_ROW + j, line * depth + to]
                for t in range(tall):
                    piece = land_a[q][a][group * tall + t, i]
                    if k:
                        send_b[q, k - 1, j, t] = piece
                    else:
                        blocks[j, t, place, core, :, cut(q)] = piece
            if k:
                remote(
                    send_b.at[q, k - 1], blocks.at[:, :, place, core, :, cut(q)],
                    b_s.at[q * depth + k], b_r.at[q * depth + k], at(line, to),
                ).start()

    out_order = [(q, a, pair) for q in range(SPLIT) for a, pair in enumerate(p.out_steps)]
    for at_step in range(len(out_order) + AHEAD):
        if at_step % pairs == min(2, pairs - 1) and at_step // pairs + 1 < SPLIT:
            add(at_step // pairs + 1)
        if at_step < len(out_order):
            across(*out_order[at_step])
        if at_step >= AHEAD:
            along(*out_order[at_step - AHEAD])

    for q, _, pair in out_order:
        for k in pair:
            rows = blocks.at[:, :, behind[k], core, :, cut(q)]
            sem = q * depth + k
            if k:
                landed(rows, b_r.at[sem])
            remote(rows, rows, x_s.at[sem], x_r.at[sem], partner).start()
    for q, _, pair in out_order:
        for k in pair:
            landed(blocks.at[:, :, behind[k], far_core, :, cut(q)], x_r.at[q * depth + k])

    share = slots // 2
    assert share == 2

    @pl.loop(0, 2)
    def _(turn):
        first = lax.rem(turn + far_core, 2) * share
        both = [first, first + 1]
        for j in both:
            landed(stat.at[j], load_o.at[j])

        def statistics(dims):
            for j in both:
                g = blocks[j].reshape(block, block)
                stat[j] = DECAY_RATE * stat[j] + dot(g, g, dims)
                pltpu.make_async_copy(stat.at[j], new.at[0, j], save_n.at[j]).start()

        pl.when(core == 0)(lambda: statistics(((1,), (1,))))
        pl.when(core == 1)(lambda: statistics(((0,), (0,))))

        def each(f, *lists):
            return [f(*values) for values in zip(*lists)]

        a = [stat[j] for j in both]
        norm2 = each(
            lambda a: jnp.sum(jnp.sum(a * a, axis=0, keepdims=True), axis=1, keepdims=True) + EPSILON, a
        )
        norm = each(jnp.sqrt, norm2)
        inverse = each(lambda n: 1.0 / n, norm)
        b1 = each(lambda a, v: (a * v).astype(BF16), a, inverse)
        m2 = each(dot, b1, b1)
        b2 = each(lambda m: m.astype(BF16), m2)
        m3 = each(dot, b1, b2)
        b3 = each(lambda m: m.astype(BF16), m3)
        c4, c5, c6 = (jnp.asarray(v, BF16) for v in COEF[4:])
        upper = each(lambda x, y, w: c4 * x + c5 * y + c6 * w, b1, b2, b3)
        high = each(dot, b3, upper)
        low = each(
            lambda a, v, m2, m3: (COEF[1] * v) * a + COEF[2] * m2 + COEF[3] * m3 + eye[...],
            a, inverse, m2, m3,
        )
        x = each(lambda h, l, n: ((h + l) * lax.rsqrt(jnp.sqrt(n))).astype(BF16), high, low, norm)
        for j, value in zip(both, x):
            root[j] = value.reshape(root.shape[1:])

        @pl.when(turn == 0)
        def _():
            for i, j in enumerate(both):
                remote(root.at[j], other.at[i], root_s.at[i], root_r.at[i], partner).start()

    def apply(j, left, right):
        g = blocks[j].reshape(block, block)
        part = dot(g, right.reshape(block, block)).astype(BF16)
        return dot(left.reshape(block, block), part).astype(BF16).reshape(whole.shape[1:])

    matrix_id = lax.broadcasted_iota(jnp.int32, sums.shape[1:], 0)
    for i in range(share):
        j = core * share + i
        landed(other.at[i], root_r.at[i])

        @pl.when(core == 0)
        def _():
            whole[i] = apply(j, root[j], other[i])

        @pl.when(core == 1)
        def _():
            whole[i] = apply(j, other[i], root[j])

        remote(whole.at[i, :, :, far_core], half_out.at[j], p_s.at[i], p_r.at[i], partner).start()
        half_out[j] = whole[i, :, :, core]
        value = whole[i].reshape(block, block).astype(F32)
        total = fold(value * value)
        sums[1] = sums[1] + jnp.where(matrix_id == tab[p.matrix_row + j, me], total, 0.0)
    for i in range(share):
        landed(half_out.at[far_core * share + i], p_r.at[i])

    sums_z[place] = sums[...]

    @pl.loop(1, depth)
    def _(step):
        remote(sums, sums_z.at[place], qz_s, qz_r, at(line, lax.rem(place + step, depth))).start()

    back_order = [(q, a, pair) for q in range(SPLIT) for a, pair in enumerate(p.back_steps)]
    for q, _, pair in back_order:
        for k in pair:
            if k:
                to, sem = behind[k], q * depth + k
                remote(
                    half_out.at[:, :, to, :, cut(q)], land_c[q][k - 1], c_s.at[sem], c_r.at[sem], at(line, to)
                ).start()

    def back_across(q, a, pair):
        for k in pair:
            if k:
                landed(land_c[q][k - 1], c_r.at[q * depth + k])

        @pl.loop(0, lines, unroll=4)
        def _(to):
            for i, k in enumerate(pair):
                slot = tab[SLOT_ROW + lax.div(to, tall), line * depth + ahead[k]]
                if k:
                    send_d[q][a][to, i] = land_c[q][k - 1][slot, lax.rem(to, tall)]
                else:
                    send_d[q][a][to, i] = half_out[slot, lax.rem(to, tall), place, :, cut(q)]

        spot = pl.ds(p.start[a] + line * len(pair), len(pair))

        @pl.loop(1, lines, unroll=5)
        def _(step):
            to = lax.rem(line + step, lines)
            remote(
                send_d[q][a].at[to], land_d[q].at[spot],
                d_s.at[q * pairs + a], d_r.at[q * pairs + a], at(to, place),
            ).start()

        land_d[q][spot] = send_d[q][a][line]

    def back_pair(q, a, pair):
        sem = q * pairs + a
        landed(land_d[q].at[pl.ds(0, (lines - 1) * len(pair))], d_r.at[sem])
        rows = pl.ds(p.start[a], lines * len(pair))
        remote(land_d[q].at[rows], land_e[q].at[rows], y_s.at[sem], y_r.at[sem], partner).start()

    def far_landed(q):
        for a, pair in enumerate(p.back_steps):
            rows = pl.ds(p.start[a], lines * len(pair))
            landed(land_e[q].at[rows], y_r.at[q * pairs + a])

    def place_rows(q, h, source, m):
        factor = scales[pl.ds(m, 1), :]
        rows = pl.ds(pl.multiple_of(h * half, half), half)
        for c in range(columns):
            piece = source[q][tab[p.land_row + m * columns + c, 0]].astype(F32) * factor
            made[m, rows, cut(q, c)] = piece.astype(BF16)

    def place_both(q):
        far_landed(q)

        @pl.loop(0, p.matrices)
        def _(m):
            place_rows(q, core, land_d, m)
            place_rows(q, far_core, land_e, m)

    def find_scales():
        landed(sums_c.at[1], qc_r)
        total = jnp.sum(sums_c[0] + sums_c[1], axis=2, keepdims=True)
        count = float(p.slab * p.fsdp * p.model)
        scale = jnp.sqrt((total[0] / count + EPSILON) / (total[1] / count + EPSILON))
        scales[...] = jnp.broadcast_to(scale, scales.shape)

    for a in range(len(back_order) + AHEAD):
        if a < len(back_order):
            back_across(*back_order[a])
        if a == 1:
            landed(sums_z.at[pl.ds(0, depth - 1)], qz_r)
            sums_l[line] = jnp.sum(sums_z[...], axis=0)

            @pl.loop(1, lines)
            def _(step):
                remote(sums_l.at[line], sums_l.at[line], ql_s, ql_r, at(lax.rem(line + step, lines), place)).start()

        if a == pairs - 1:
            landed(sums_l.at[pl.ds(0, lines - 1)], ql_r)
            sums_c[0] = jnp.sum(sums_l[...], axis=0)
            remote(sums_c.at[0], sums_c.at[1], qc_s, qc_r, partner).start()
        if a == len(back_order) + AHEAD - 1:
            find_scales()
            for q in range(SPLIT - 1):
                place_both(q)
        if a >= AHEAD:
            back_pair(*back_order[a - AHEAD])

    last = SPLIT - 1

    @pl.loop(0, p.matrices)
    def _(m):
        place_rows(last, core, land_d, m)

    far_landed(last)

    @pl.loop(0, p.matrices)
    def _(m):
        place_rows(last, far_core, land_e, m)
        pltpu.make_async_copy(made.at[m], upd.at[m], save_u.at[m]).start()

    for q in range(SPLIT):
        landed(theirs.at[pl.ds(0, part_of)], pair_s.at[q])
        for a, pair in enumerate(p.out_steps):
            landed(send_a[q][a].at[pl.ds(0, lines - 1)], a_s.at[q * pairs + a])
        for a, pair in enumerate(p.back_steps):
            landed(send_d[q][a].at[pl.ds(0, lines - 1)], d_s.at[q * pairs + a])
            landed(land_d[q].at[pl.ds(p.start[a], lines * len(pair))], y_s.at[q * pairs + a])
        for k in range(depth):
            landed(blocks.at[:, :, behind[k], core, :, cut(q)], x_s.at[q * depth + k])
            if k:
                landed(send_b.at[q, k - 1], b_s.at[q * depth + k])
                landed(land_c[q][k - 1], c_s.at[q * depth + k])
    for j in range(slots):
        landed(stat.at[j], save_n.at[j])
    for i in range(share):
        landed(root.at[i], root_s.at[i])
        landed(whole.at[i, :, :, far_core], p_s.at[i])
    landed(sums_z.at[pl.ds(0, depth - 1)], qz_s)
    landed(sums_l.at[pl.ds(0, lines - 1)], ql_s)
    landed(sums_c.at[0], qc_s)
    for m in range(p.matrices):
        landed(made.at[m], save_u.at[m])


def tables(p, owner, me, line, place):
    groups, columns, lines, depth = p.groups, p.columns, p.lines, p.depth

    def bits(n):
        assert n & (n - 1) == 0
        return n.bit_length() - 1

    group = lax.shift_right_logical(owner, bits(columns)) & (groups - 1)
    matrix = lax.shift_right_logical(owner, bits(columns * groups))
    local = matrix * columns + (owner & (columns - 1))
    code = jnp.zeros((1, p.fsdp), jnp.int32)
    for j in range(p.slots):
        here = group[j : j + 1] == lax.div(me, p.span)
        code = code + jnp.where(here, local[j : j + 1] + 1, 0)
    group_id = lax.broadcasted_iota(jnp.int32, (groups, p.fsdp), 0)
    slot = jnp.zeros((groups, p.fsdp), jnp.int32)
    for j in range(1, p.slots):
        slot = slot + jnp.where(group[j : j + 1] == group_id, j, 0)
    lane = lax.broadcasted_iota(jnp.int32, (1, p.fsdp), 1)
    gap = ((lane & (depth - 1)) - place) & (depth - 1)
    land = jnp.zeros((1, p.fsdp), jnp.int32)
    for a, pair in enumerate(p.back_steps):
        for i, k in enumerate(pair):
            spot = p.start[a] + lax.shift_right_logical(lane, bits(depth)) * len(pair) + i
            land = land + jnp.where(gap == k, spot, 0)
    block_id = lax.broadcasted_iota(jnp.int32, (p.matrices * columns, p.fsdp), 0)
    hit = jnp.where(code == block_id + 1, land, 0)
    hit = jnp.broadcast_to(jnp.sum(hit, axis=1, keepdims=True), hit.shape)
    return [
        (0, jnp.clip(code - 1, 0, p.matrices * columns - 1)),
        (GROUP_ROW, group),
        (SLOT_ROW, jnp.minimum(slot, p.slots - 1)),
        (p.land_row, jnp.minimum(hit, lines * depth - 1)),
        (p.matrix_row, matrix),
    ]


def body(p, gradient, old_stats, owner_table):
    depth, lines, slots, block = p.depth, p.lines, p.slots, p.block
    half, tall, wide = p.half, p.tall, p.wide
    pairs, steps = SPLIT * p.pairs, SPLIT * depth
    dma = pltpu.SemaphoreType.DMA
    vm = pltpu.VMEM
    full = (slots, tall, depth, 2, half, block)

    def chunks(order):
        return [[vm((lines, len(pair), half, wide), BF16) for pair in order] for _ in range(SPLIT)]

    scratch = [
        vm((p.matrices, half, p.model), BF16),
        vm((p.matrices, half, p.model), BF16),
        [vm((p.matrices * p.columns, half, wide), BF16) for _ in range(SPLIT)],
        chunks(p.out_steps),
        chunks(p.out_steps),
        vm((SPLIT, depth - 1, slots, tall, half, wide), BF16),
        vm(full, BF16),
        vm((block, block), F32),
        vm(full, BF16),
        vm((2,) + full[1:], BF16),
        vm((slots, tall, depth, half, block), BF16),
        [[vm((slots, tall, half, wide), BF16) for _ in range(depth - 1)] for _ in range(SPLIT)],
        chunks(p.back_steps),
        [vm((lines * depth, half, wide), BF16) for _ in range(SPLIT)],
        vm((2, p.matrices, 128), F32),
        vm((p.matrices, wide), F32),
        vm((depth, 2, p.matrices, 128), F32),
        vm((lines, 2, p.matrices, 128), F32),
        vm((2, 2, p.matrices, 128), F32),
        vm((p.table_rows, p.fsdp), jnp.int32),
        pltpu.SMEM((p.table_rows, p.fsdp), jnp.int32),
        vm((slots, block, block), F32),
        vm((p.matrices, p.slab, p.model), BF16),
        vm((slots, p.fsdp), jnp.int32),
        vm((2,) + full[1:], BF16),
        [vm((lines * depth, half, wide), BF16) for _ in range(SPLIT)],
    ]
    counts = [SPLIT, slots, slots, p.matrices, SPLIT, SPLIT, pairs, pairs, steps, steps]
    counts += [steps, steps, 2, 2, steps, steps, pairs, pairs, pairs, pairs]
    scratch += [dma((count,)) for count in counts]
    scratch += [dma] * 8 + [dma((2,))] * 2
    update, fresh = pl.pallas_call(
        functools.partial(kernel, p),
        out_shape=(
            jax.ShapeDtypeStruct((p.matrices, p.slab, p.model), BF16),
            jax.ShapeDtypeStruct(old_stats.shape, F32),
        ),
        in_specs=[
            pl.BlockSpec(memory_space=pltpu.HBM),
            pl.BlockSpec(memory_space=pltpu.HBM),
            pl.BlockSpec(memory_space=pltpu.HBM),
        ],
        out_specs=(pl.BlockSpec(memory_space=pl.ANY), pl.BlockSpec(memory_space=pl.ANY)),
        scratch_shapes=scratch,
        compiler_params=pltpu.CompilerParams(
            collective_id=0, has_side_effects=True, vmem_limit_bytes=VMEM_BYTES
        ),
        name="shampoo",
    )(*(pltpu.with_memory_space_constraint(x, pltpu.HBM) for x in (owner_table.T, gradient, old_stats)))
    return update, fresh


def solution(mesh):
    def whole(gradient, old_stats, owner_table):
        fsdp = mesh.shape["fsdp"]
        _, matrices, rows, model = gradient.shape
        p = Plan(fsdp, matrices, rows // fsdp, model, owner_table.shape[1], old_stats.shape[2])
        return jax.shard_map(
            functools.partial(body, p),
            mesh=mesh,
            in_specs=(P("rep", None, "fsdp", None), P("rep", "fsdp", None, None), P()),
            out_specs=(P(None, "fsdp", None), P("rep", "fsdp", None, None)),
            check_vma=False,
        )(gradient, old_stats, owner_table)

    return whole
```
